128 devices in a mesh: row: 8 (over z, core), col: 16 (over y, x).
Axes of the slice: x: 4, y: 4, z: 4, core: 2. Of those that a mesh axis runs over, the one named last changes fastest.
Arguments:
- atoms: bfloat16 [32768, 128], P(('row', 'col')), may hold values from -6 to 6
- atom_bias: bfloat16 [32768, 4, 128], P(('row', 'col')), may hold values from -10 to 400
- key_mask: int32 [1024, 128], P(('row', 'col')), may hold values 0 or 1
- atom_token: int32 [32768], P(('row', 'col')), may hold values from 0 to 4095, as said below
- tokens: bfloat16 [4096, 768], P('row'), may hold values from -6 to 6
- pair_bias: bfloat16 [16, 4096, 4096], P(None, 'row', 'col'), may hold values from -10 to 400
- token_mask: int32 [4096], P('col'), may hold values from 0 to 1, as said below
- atom_query: bfloat16 [128, 128], replicated, may hold values from -0.5 to 0.5
- atom_keyval: bfloat16 [128, 256], replicated, may hold values from -0.5 to 0.5
- atom_gate: bfloat16 [128, 128], replicated, may hold values from -0.5 to 0.5
- atom_out: bfloat16 [128, 128], replicated, may hold values from -0.5 to 0.5
- pool_weight: bfloat16 [128, 768], replicated, may hold values from -0.5 to 0.5
- token_query: bfloat16 [768, 768], replicated, may hold values from -0.21875 to 0.21875
- token_keyval: bfloat16 [768, 1536], replicated, may hold values from -0.21875 to 0.21875
- token_gate: bfloat16 [768, 768], replicated, may hold values from -0.21875 to 0.21875
- token_out: bfloat16 [768, 768], replicated, may hold values from -0.21875 to 0.21875
- trans_gate: bfloat16 [768, 1536], replicated, may hold values from -0.21875 to 0.21875
- trans_up: bfloat16 [768, 1536], replicated, may hold values from -0.21875 to 0.21875
- trans_down: bfloat16 [1536, 768], replicated, may hold values from -0.15625 to 0.15625
- back_weight: bfloat16 [768, 128], replicated, may hold values from -0.21875 to 0.21875
Outputs:
- atoms_new: bfloat16 [32768, 128], P(('row', 'col'))
- tokens_new: bfloat16 [4096, 768], P('row')
The draws below stay inside these ranges and needn't reach their ends.
Inputs may be any that keep to these rules, and one draw needn't show every extreme that they name: atom_token never falls along the atoms; the atoms of block r of 4096 atoms name exactly the tokens of block r of 512 tokens, each at least once. `token_mask`: 1 on a prefix of 2048 tokens or more, 0 after it; the last token is 0.
All inputs are finite; a program needn't handle non-finite values. No bound on the sum of `key_mask` on one device may be relied on, other than what follows from the above.
Results may differ from the reference program's by a relative error of at most 0.013.
Values may be sent and summed in bfloat16 or wider, within the bound.
A program may use at most 128 MiB of HBM per device.

```python
import jax
import jax.numpy as jnp
from jax import lax

CA = 128
HA = 4
DA = 32
WQ = 32
WK = 128
CT = 768
HT = 16
DT = 48
FT = 1536
TOK_ROW = 512
TOKENS = 4096
ATOMS = 32768
ATOMS_ROW = 4096
WINDOWS = 1024


def draw_atom_bias(key, part):
    key = jax.random.fold_in(key, 3)
    key_base = jax.random.fold_in(key, 0)
    base = jnp.clip(2.5 * jax.random.normal(key_base, (ATOMS, HA, WK), jnp.float32), -10.0, 10.0)
    return base.astype(jnp.bfloat16)


def draw_pair_bias(key, part):
    key = jax.random.fold_in(key, 7)
    key_base = jax.random.fold_in(key, 0)
    base = jnp.clip(2.5 * jax.random.normal(key_base, (HT, TOKENS, TOKENS), jnp.float32), -10.0, 10.0)
    return base.astype(jnp.bfloat16)


def draw_atom_token(key, part):
    key = jax.random.fold_in(key, 11)
    blocks = ATOMS // ATOMS_ROW

    def one_block(sub_key):
        cuts = jax.random.permutation(sub_key, ATOMS_ROW - 1)[:TOK_ROW - 1] + 1
        marks = jnp.zeros((ATOMS_ROW,), jnp.int32).at[cuts].set(1)
        return jnp.cumsum(marks).astype(jnp.int32)
    local = jax.vmap(one_block)(jax.random.split(key, blocks))
    offsets = (jnp.arange(blocks, dtype=jnp.int32) * TOK_ROW)[:, None]
    return (local + offsets).reshape(ATOMS).astype(jnp.int32)


def draw_token_mask(key, part):
    key = jax.random.fold_in(key, 13)
    live_count = jax.random.randint(key, (), TOKENS // 2, TOKENS)
    return (jnp.arange(TOKENS, dtype=jnp.int32) < live_count).astype(jnp.int32)


def with_ends(entries, key, low, high):
    spot = [jax.random.randint(jax.random.fold_in(key, axis), (), 0, length) for axis, length in enumerate(entries.shape)]
    main_axis = entries.shape.index(max(entries.shape))
    beside = spot[:main_axis] + [(spot[main_axis] + 1) % entries.shape[main_axis]] + spot[main_axis + 1:]
    return entries.at[tuple(spot)].set(low).at[tuple(beside)].set(high)


def shard_levels(own_key, shape, cuts, smallest, largest):
    loudness, own = 1.0, jax.random.fold_in(own_key, 6)
    for dim, blocks in cuts:
        heights = jnp.exp(jax.random.uniform(jax.random.fold_in(own, dim), (blocks,), jnp.float32, smallest / len(cuts), largest / len(cuts)))
        loudness = loudness * jnp.repeat(heights, shape[dim] // blocks).reshape([-1 if axis == dim else 1 for axis in range(len(shape))])
    return loudness


def bell_draw(stream_key, extent, width, limit, cuts=(), kind=jnp.bfloat16):
    loudness = shard_levels(stream_key, extent, cuts, -0.22, 0.18) if cuts else 1.0
    result = jax.random.normal(stream_key, extent, jnp.float32) * width * loudness
    return jnp.minimum(jnp.maximum(result, -limit), limit).astype(kind)


def setup_inputs(seed: int = 0) -> dict:
    splits = jax.random.split(jax.random.key(seed), 21)
    atoms = bell_draw(splits[0], (ATOMS, CA), 1.0, 6.0, ((0, 128),))
    atom_bias = draw_atom_bias(jax.random.fold_in(splits[20], 71), 0)
    key_mask = with_ends((jax.random.randint(splits[2], (WINDOWS, WK), 0, 8) < 7).astype(jnp.int32), jax.random.fold_in(splits[2], 1), 0, 1)
    atom_token = draw_atom_token(jax.random.fold_in(splits[20], 71), 0)
    tokens = bell_draw(splits[4], (TOKENS, CT), 1.0, 6.0, ((0, 8),))
    pair_bias = draw_pair_bias(jax.random.fold_in(splits[20], 71), 0)
    token_mask = draw_token_mask(jax.random.fold_in(splits[20], 71), 0)
    atom_query = bell_draw(splits[7], (CA, CA), CA ** -0.5, 0.5)
    atom_keyval = bell_draw(splits[8], (CA, 2 * CA), CA ** -0.5, 0.5)
    atom_gate = bell_draw(splits[9], (CA, CA), CA ** -0.5, 0.5)
    atom_out = bell_draw(splits[10], (CA, CA), CA ** -0.5, 0.5)
    pool_weight = bell_draw(splits[11], (CA, CT), CA ** -0.5, 0.5)
    token_query = bell_draw(splits[12], (CT, CT), CT ** -0.5, 0.21875)
    token_keyval = bell_draw(splits[13], (CT, 2 * CT), CT ** -0.5, 0.21875)
    token_gate = bell_draw(splits[14], (CT, CT), CT ** -0.5, 0.21875)
    token_out = bell_draw(splits[15], (CT, CT), CT ** -0.5, 0.21875)
    trans_gate = bell_draw(splits[16], (CT, FT), CT ** -0.5, 0.21875)
    trans_up = bell_draw(splits[17], (CT, FT), CT ** -0.5, 0.21875)
    trans_down = bell_draw(splits[18], (FT, CT), FT ** -0.5, 0.15625)
    back_weight = bell_draw(splits[19], (CT, CA), CT ** -0.5, 0.21875)
    return {"atoms": atoms, "atom_bias": atom_bias, "key_mask": key_mask, "atom_token": atom_token, "tokens": tokens, "pair_bias": pair_bias, "token_mask": token_mask, "atom_query": atom_query, "atom_keyval": atom_keyval, "atom_gate": atom_gate, "atom_out": atom_out, "pool_weight": pool_weight, "token_query": token_query, "token_keyval": token_keyval, "token_gate": token_gate, "token_out": token_out, "trans_gate": trans_gate, "trans_up": trans_up, "trans_down": trans_down, "back_weight": back_weight}


EPSILON = 1e-05
MASKED = -1000000000.0

def normalize(values):
    average = lax.optimization_barrier(jnp.mean(values, axis=-1, keepdims=True))
    centred = values - average
    variance = lax.optimization_barrier(jnp.mean(centred * centred, axis=-1, keepdims=True))
    return centred * lax.rsqrt(variance + EPSILON)

def product(left, right):
    return jnp.dot(left, right, preferred_element_type=jnp.float32)

def stored(values):
    return lax.optimization_barrier(values.astype(jnp.bfloat16)).astype(jnp.float32)

def reference(atoms, atom_bias, key_mask, atom_token, tokens, pair_bias, token_mask, atom_query, atom_keyval, atom_gate, atom_out, pool_weight, token_query, token_keyval, token_gate, token_out, trans_gate, trans_up, trans_down, back_weight):
    windows = ATOMS // WQ
    reach = (WK - WQ) // 2
    atom_norm = normalize(atoms.astype(jnp.float32)).astype(jnp.bfloat16)
    atom_queries = stored(product(atom_norm, atom_query))
    atom_kv = product(atom_norm, atom_keyval).astype(jnp.bfloat16)
    padded = jnp.pad(atom_kv, ((reach, reach), (0, 0)))
    slot_index = (WQ * jnp.arange(windows)[:, None] + jnp.arange(WK)[None, :]).astype(jnp.int32)
    neighbours = padded[slot_index].astype(jnp.float32)
    key_part = neighbours[:, :, :CA].reshape(windows, WK, HA, DA)
    value_part = neighbours[:, :, CA:].reshape(windows, WK, HA, DA)
    query_part = atom_queries.reshape(windows, WQ, HA, DA)
    position = slot_index - reach
    valid = (key_mask == 1) & (position >= 0) & (position < ATOMS)
    scores = jnp.einsum('wqhd,wkhd->whqk', query_part, key_part, precision=lax.Precision.HIGHEST) * DA ** (-0.5)
    scores = scores + atom_bias.astype(jnp.float32).reshape(windows, WQ, HA, WK).transpose(0, 2, 1, 3)
    scores = jnp.where(valid[:, None, None, :], scores, MASKED)
    expo = jnp.exp(scores - lax.optimization_barrier(jnp.max(scores, axis=-1, keepdims=True)))
    total = lax.optimization_barrier(jnp.sum(expo, axis=-1, keepdims=True))
    weights = stored(expo)
    attended = jnp.einsum('whqk,wkhd->wqhd', weights, value_part, precision=lax.Precision.HIGHEST) / total.transpose(0, 2, 1, 3)
    gating = jax.nn.sigmoid(product(atom_norm, atom_gate))
    atom_attended = (attended.reshape(ATOMS, CA) * gating).astype(jnp.bfloat16)
    atoms_mid = (atoms.astype(jnp.float32) + product(atom_attended, atom_out)).astype(jnp.bfloat16)
    features = jax.nn.relu(product(atoms_mid, pool_weight)).astype(jnp.bfloat16)
    token_sums = jax.ops.segment_sum(features.astype(jnp.float32), atom_token, num_segments=TOKENS)
    token_counts = jax.ops.segment_sum(jnp.ones((ATOMS,), jnp.float32), atom_token, num_segments=TOKENS)
    tokens_mid = (tokens.astype(jnp.float32) + token_sums / token_counts[:, None]).astype(jnp.bfloat16)
    token_norm = normalize(tokens_mid.astype(jnp.float32)).astype(jnp.bfloat16)
    queries = stored(product(token_norm, token_query)).reshape(TOKENS, HT, DT).transpose(1, 0, 2)
    keyval = stored(product(token_norm, token_keyval))
    keys_all = keyval[:, :CT].reshape(TOKENS, HT, DT).transpose(1, 0, 2)
    values_all = keyval[:, CT:].reshape(TOKENS, HT, DT).transpose(1, 0, 2)
    live = token_mask == 1

    def one_head(operands):
        head_queries, head_keys, head_values, head_bias = operands
        head_scores = jnp.dot(head_queries, head_keys.T, precision=lax.Precision.HIGHEST) * DT ** (-0.5)
        head_scores = head_scores + head_bias.astype(jnp.float32)
        head_scores = jnp.where(live[None, :], head_scores, MASKED)
        head_exp = jnp.exp(head_scores - lax.optimization_barrier(jnp.max(head_scores, axis=-1, keepdims=True)))
        head_total = lax.optimization_barrier(jnp.sum(head_exp, axis=-1, keepdims=True))
        return jnp.dot(stored(head_exp), head_values, precision=lax.Precision.HIGHEST) / head_total
    heads_out = lax.map(one_head, (queries, keys_all, values_all, pair_bias))
    attended_tok = heads_out.transpose(1, 0, 2).reshape(TOKENS, CT)
    token_attended = (attended_tok * jax.nn.sigmoid(product(token_norm, token_gate))).astype(jnp.bfloat16)
    tokens_att = (tokens_mid.astype(jnp.float32) + product(token_attended, token_out)).astype(jnp.bfloat16)
    trans_norm = normalize(tokens_att.astype(jnp.float32)).astype(jnp.bfloat16)
    trans_hidden = (jax.nn.silu(product(trans_norm, trans_gate)) * product(trans_norm, trans_up)).astype(jnp.bfloat16)
    tokens_new = (tokens_att.astype(jnp.float32) + product(trans_hidden, trans_down)).astype(jnp.bfloat16)
    token_update = product(tokens_new, back_weight).astype(jnp.bfloat16)
    atoms_new = (atoms_mid.astype(jnp.float32) + token_update[atom_token].astype(jnp.float32)).astype(jnp.bfloat16)
    return (atoms_new, tokens_new)
```

```python
import jax
import jax.numpy as jnp
from jax import lax
from jax.experimental import pallas as pl
from jax.experimental.pallas import tpu as pltpu
from jax.sharding import PartitionSpec as P

F32 = jnp.float32
BF16 = jnp.bfloat16
MESH = pl.DeviceIdType.MESH
ROWS, COLS = 8, 16
EPSILON = 1e-05
MASKED = -1000000000.0
HA, DA, WQ, WK = 4, 32, 32, 128
DT = 48
REACH = 48
A = 256
T = 512
K = 256
C = 768
G = 384
OWN = 32
PARTS = 4
H = 128
TOTAL_ATOMS = 32768


def dot(a, b):
    return jnp.dot(a, b, preferred_element_type=F32)


def norm(x):
    mean = jnp.mean(x, axis=-1, keepdims=True)
    d = x - mean
    var = jnp.mean(d * d, axis=-1, keepdims=True)
    return d * lax.rsqrt(var + EPSILON)


def sigmoid(x):
    return 1.0 / (1.0 + jnp.exp(-x))


def iota(shape, dim):
    return lax.broadcasted_iota(jnp.int32, shape, dim)


IN_NAMES = (
    "atoms", "abias", "kmask", "atok", "tokens", "pbias", "tmask", "aq", "akv", "ag", "ao", "pool",
    "tq", "tkv", "tg", "to", "rg", "ru", "rd", "back",
)
EARLY = ("atoms", "akv", "aq", "ag", "kmask", "abias", "ao", "atok", "pool")
LATE = ("tokens", "tg", "tq", "tkv", "tmask", "pbias", "to", "rg", "ru", "rd", "back")
SPANS = tuple(((DT * h) // 128, (DT * h + DT - 1) // 128 - (DT * h) // 128 + 1) for h in range(8))


def split_lse(stat):
    high = stat.astype(BF16).astype(F32)
    rest = stat - high
    middle = rest.astype(BF16).astype(F32)
    third = iota(stat.shape, 1) // 8
    return jnp.where(third == 0, high, jnp.where(third == 1, middle, rest - middle))


def merge(blocks, want_lse):
    l_r, l_c = iota((128, 128), 0), iota((128, 128), 1)
    join = jnp.where((l_r < 24) & (lax.rem(l_r, 8) == lax.rem(l_c, 8)), 1.0, 0.0).astype(BF16)
    s_r, s_c = iota((128, G), 0), iota((128, G), 1)
    spread = jnp.where((s_r < 16) & (lax.rem(s_r, 8) == s_c // DT), 1.0, 0.0).astype(BF16)
    lse = [dot(b[:, G:], join) for b in blocks]
    top = lse[0]
    for l in lse[1:]:
        top = jnp.maximum(top, l)
    wgt = [jnp.exp(l - top) for l in lse]
    total = wgt[0]
    for w in wgt[1:]:
        total = total + w
    inv = 1.0 / total
    first = iota(top.shape, 1) < 8
    out = None
    for w, b in zip(wgt, blocks):
        w = w * inv
        high = w.astype(BF16).astype(F32)
        term = dot(jnp.where(first, high, w - high).astype(BF16), spread) * b[:, :G].astype(F32)
        out = term if out is None else out + term
    if want_lse:
        return jnp.concatenate([out, split_lse(top + jnp.log(total))], axis=1).astype(BF16)
    return out


def kernel(*refs):
    n_in = len(IN_NAMES)
    hbm = dict(zip(IN_NAMES, refs[:n_in]))
    atoms_out, tokens_out = refs[n_in : n_in + 2]
    (
        ext, abias, kmask, tk, tokens, pbias, tmask, aq, akv, ag, ao, pool, tq, tkv, tg, to, rg, ru, rd, back,
        g_mid, feats, acc, selsum, tmid, tnorm, knorm, q_s, kt_s, v_s, snd, rcv, snd2, rcv2, g_new, g_upd,
        in_sem, halo_s, halo_r, tok_s, tok_r, mid_s, mid_r, key_s, key_r,
        one_s, one_r, two_s, two_r, upd_s, upd_r, new_s, new_r, own_sem,
    ) = refs[n_in + 2 :]

    r = lax.axis_index("row")
    c = lax.axis_index("col")
    y, x = c // 4, lax.rem(c, 4)
    z, core = r // 2, lax.rem(r, 2)
    lin = r * COLS + c
    nxt = lax.rem(lin + 1, ROWS * COLS)
    prv = lax.rem(lin + ROWS * COLS - 1, ROWS * COLS)
    nxt_id = (nxt // COLS, lax.rem(nxt, COLS))
    prv_id = (prv // COLS, lax.rem(prv, COLS))
    sibling = (z * 2 + 1 - core, c)

    def remote(src, dst, ss, rs, dev):
        return pltpu.make_async_remote_copy(
            src_ref=src, dst_ref=dst, send_sem=ss, recv_sem=rs, device_id=dev, device_id_type=MESH
        )

    def col_peer(i):
        return lax.rem(c + i, COLS)

    def x_peer(i):
        return y * 4 + lax.rem(x + i, 4)

    def y_peer(i):
        return lax.rem(y + i, 4) * 4 + x

    near = (x_peer, y_peer)

    bar = pltpu.get_barrier_semaphore()
    for dev in (nxt_id, prv_id, sibling, (lax.rem(z + 1, 4) * 2 + core, c), (lax.rem(z + 3, 4) * 2 + core, c)):
        pl.semaphore_signal(bar, inc=1, device_id=dev, device_id_type=MESH)
    for i in range(1, COLS):
        pl.semaphore_signal(bar, inc=1, device_id=(r, col_peer(i)), device_id_type=MESH)

    fetch = {}
    vm = dict(
        atoms=ext.at[pl.ds(REACH, A)], abias=abias, kmask=kmask, atok=tk.at[c], tokens=tokens, pbias=pbias, tmask=tmask,
        aq=aq, akv=akv, ag=ag, ao=ao, pool=pool, tq=tq, tkv=tkv, tg=tg, to=to, rg=rg, ru=ru, rd=rd, back=back,
    )
    for i, name in enumerate(EARLY + LATE):
        fetch[name] = pltpu.make_async_copy(hbm[name], vm[name], in_sem.at[i])
    for name in EARLY:
        fetch[name].start()
    pl.semaphore_wait(bar, 5 + COLS - 1)

    halo = [
        remote(hbm["atoms"].at[pl.ds(A - REACH, REACH)], ext.at[pl.ds(0, REACH)], halo_s.at[0], halo_r.at[0], nxt_id),
        remote(hbm["atoms"].at[pl.ds(0, REACH)], ext.at[pl.ds(REACH + A, REACH)], halo_s.at[1], halo_r.at[1], prv_id),
    ]
    for cp in halo:
        cp.start()

    def tok_copy(i):
        return remote(hbm["atok"], tk.at[c], tok_s.at[col_peer(i)], tok_r.at[c], (r, col_peer(i)))

    for i in range(1, COLS):
        tok_copy(i).start()
    for name in LATE:
        fetch[name].start()

    for name in ("atoms", "akv", "aq", "ag"):
        fetch[name].wait()
    own_f = ext[pl.ds(REACH, A), :].astype(F32)
    own_n = norm(own_f).astype(BF16)
    q_a = dot(own_n, aq[...]).astype(BF16)
    gate_a = sigmoid(dot(own_n, ag[...]))
    kv_own = dot(own_n, akv[...]).astype(BF16)
    fetch["kmask"].wait()
    fetch["abias"].wait()
    p_r = iota((HA * WQ, HA * WQ), 0)
    p_c = iota((HA * WQ, HA * WQ), 1)
    perm = (p_c == lax.rem(p_r, WQ) * HA + p_r // WQ).astype(F32).astype(BF16)
    bias_w = [dot(perm, abias[pl.ds(HA * WQ * w, HA * WQ), :]) for w in range(A // WQ)]
    lane = iota((1, WK), 1)
    head_f = [jnp.where((lane // DA) == h, 1.0, 0.0).astype(F32) for h in range(HA)]
    head_b = [f.astype(BF16) for f in head_f]
    fetch["ao"].wait()

    def mid_at(half, s):
        return g_mid.at[s, pl.ds(H * half, H)]

    def mid_copy(half, s, slot, dev):
        return remote(mid_at(half, s), mid_at(half, s), mid_s.at[half, slot], mid_r.at[half, s], (r, dev))

    def hops(half, send):
        for i in (1, 3, 2):
            send(c, i - 1, near[half](i), None)
        for i in (1, 3, 2):
            send(c, i + 2, near[1 - half](i), None)
        for k, j in enumerate((1, 3, 2)):
            s = near[half](j)
            for i in (1, 3, 2):
                send(s, 3 * k + i + 5, near[1 - half](i), i == 1)

    for half in range(2):
        halo[half].wait_recv()
        edge = norm(ext[pl.ds((REACH + A) * half, REACH), :].astype(F32)).astype(BF16)
        inside = jnp.where(lin == (ROWS * COLS - 1) * half, 0.0, 1.0).astype(F32)
        edge = (dot(edge, akv[...]) * inside).astype(BF16)
        if half == 0:
            kv = jnp.concatenate([edge, kv_own[: H + REACH]], axis=0)
        else:
            kv = jnp.concatenate([kv_own[H - REACH :], edge], axis=0)
        attended = []
        for w in range(4):
            ww = 4 * half + w
            q_w = q_a[WQ * ww : WQ * (ww + 1)]
            q_bd = jnp.concatenate([q_w * head_b[h] for h in range(HA)], axis=0)
            k_w = kv[WQ * w : WQ * w + WK, :WK]
            v_w = kv[WQ * w : WQ * w + WK, WK:]
            s = lax.dot_general(q_bd, k_w, (((1,), (1,)), ((), ())), preferred_element_type=F32)
            s = s * (DA**-0.5) + bias_w[ww]
            pos = lin * A + WQ * ww + lane - REACH
            valid = (kmask[pl.ds(ww, 1), :] == 1) & (pos >= 0) & (pos < TOTAL_ATOMS)
            s = jnp.where(valid, s, MASKED)
            e = jnp.exp(s - jnp.max(s, axis=-1, keepdims=True))
            t = jnp.sum(e, axis=-1, keepdims=True)
            o = dot(e.astype(BF16), v_w) / t
            attended.append(sum(o[WQ * h : WQ * (h + 1)] * head_f[h] for h in range(HA)))
        rows = slice(H * half, H * (half + 1))
        attended = jnp.concatenate(attended, axis=0) * gate_a[rows]
        g_mid[c, rows, :] = (own_f[rows] + dot(attended.astype(BF16), ao[...])).astype(BF16)

        def first(s, slot, dev, arrives):
            if arrives is None:
                mid_copy(half, s, slot, dev).start()

        hops(half, first)

    fetch["pool"].wait()
    fetch["atok"].wait()
    for i in range(1, COLS):
        s = col_peer(i)
        remote(hbm["atok"], tk.at[s], tok_s.at[s], tok_r.at[s], (r, s)).wait_recv()
    for half in range(2):

        def onward(s, slot, dev, arrives):
            if arrives is None:
                return
            if arrives:
                mid_copy(half, s, slot, dev).wait_recv()
            mid_copy(half, s, slot, dev).start()

        hops(half, onward)

    key_off = lax.rem(c, 2) * K

    def step_blocks(step):
        o = lax.rem(step * (step + 1) // 2, 4)
        a = [(lax.rem(y + o, 4) * 4 + b, 0) for b in range(4)]
        return a + [(b * 4 + lax.rem(x + o, 4), 1) for b in range(4)]

    def selector(step, off):
        base = r * T + off
        at = iota((K, H), 0)
        return [
            jnp.where(at == tk[s][:, H * half : H * (half + 1)] - base, 1.0, 0.0).astype(F32)
            for s, half in step_blocks(step)
        ]

    def pool_into(off, step, sel):
        rows = pl.ds(pl.multiple_of(off, K), K)
        count = sel[0]
        for m in sel[1:]:
            count = count + m
        selsum[rows, :] += count
        sel = jnp.concatenate([m.astype(BF16) for m in sel], axis=1)
        acc[rows, :] += dot(sel, feats[pl.ds(pl.multiple_of(step * 1024, 1024), 1024), :])

    acc[...] = jnp.zeros(acc.shape, F32)
    selsum[...] = jnp.zeros(selsum.shape, F32)

    def pool_step(step, carry):
        @pl.when(step > 0)
        def _():
            for s, half in step_blocks(step):
                mid_copy(half, s, 0, s).wait_recv()

        for n, (s, half) in enumerate(step_blocks(step)):
            f = jnp.maximum(dot(g_mid[s, pl.ds(H * half, H), :], pool[...]), 0.0).astype(BF16)
            feats[pl.ds(pl.multiple_of(step * 1024 + H * n, H), H), :] = f
        pool_into(key_off, step, selector(step, key_off))
        return carry

    lax.fori_loop(0, 4, pool_step, 0)
    fetch["tokens"].wait()
    ones = jnp.ones((H, 128), BF16)

    def finish_pool(off):
        def chunk(step, carry):
            rows = pl.ds(pl.multiple_of(off + step * 64, 64), 64)
            inv = 1.0 / dot(selsum[rows, :].astype(BF16), ones)
            inv = jnp.concatenate([inv] * (C // 128), axis=1)
            m = (tokens[rows, :].astype(F32) + acc[rows, :] * inv).astype(BF16)
            tmid[rows, :] = m
            tnorm[rows, :] = norm(m.astype(F32)).astype(BF16)
            return carry

        lax.fori_loop(0, K // 64, chunk, 0)

    finish_pool(key_off)

    z0, core0 = (c // 2) // 2, lax.rem(c // 2, 2)
    away = lax.rem(z - z0 + 4, 4)
    part = K // PARTS
    on_core = core == core0
    is_src = on_core & (away == 0)
    relays = on_core & ((away == 1) | (away == 3))
    shift = jnp.where(away == 3, 2, 0)

    def key_rows(i):
        return pl.ds(pl.multiple_of(i * part, part), part)

    def key_send(i, j):
        dev = sibling if j == 0 else (lax.rem(z + j, 4) * 2 + core, c)
        rows = pl.ds(pl.multiple_of(key_off + i * part, part), part)
        return remote(tnorm.at[rows], knorm.at[key_rows(i)], key_s.at[i, j], key_r.at[i], dev)

    def key_across(i):
        return remote(knorm.at[key_rows(i)], knorm.at[key_rows(i)], key_s.at[i, 0], key_r.at[i], sibling)

    def key_on(i):
        dev = (lax.rem(z + away, 4) * 2 + core, c)
        return remote(knorm.at[key_rows(i)], knorm.at[key_rows(i)], key_s.at[i, 1], key_r.at[i], dev)

    @pl.when(is_src)
    def _():
        for n in range(PARTS):
            key_send(n, 1).start()
            key_send((n + 2) % PARTS, 3).start()
            key_send(n, 0).start()
        knorm[...] = tnorm[pl.ds(pl.multiple_of(key_off, K), K), :]

    def other_step(step, carry):
        pool_into(K - key_off, step, selector(step, K - key_off))
        i = lax.rem(step + shift, PARTS)

        @pl.when(jnp.logical_not(is_src))
        def _():
            key_across(i).wait_recv()

        @pl.when(relays & (step < 2))
        def _():
            key_on(i).start()

        @pl.when(on_core & (away != 0))
        def _():
            key_across(i).start()

        return carry

    lax.fori_loop(0, PARTS, other_step, 0)
    finish_pool(K - key_off)
    fetch["tq"].wait()
    for i in range(4):
        q_s[pl.ds(128 * i, 128), :] = dot(tnorm[pl.ds(128 * i, 128), :], tq[...]).astype(BF16)
    own_rows = pl.ds(pl.multiple_of(c * OWN, OWN), OWN)
    fetch["tg"].wait()
    gate_t = sigmoid(dot(tnorm[own_rows, :], tg[...]))

    fetch["tkv"].wait()
    kt = (dot(knorm[...], tkv[:, :C]) * (DT**-0.5)).T
    row_i = iota((C, 1), 0)
    v_full = dot(knorm[...], tkv[:, C:])
    lane_i = iota((1, C), 1)
    for g in range(2):
        for h in range(8):
            b0, n = SPANS[h]
            lo, hi = G * g + 128 * b0, G * g + 128 * (b0 + n)
            start = G * g + DT * h
            rm = (row_i[lo:hi] >= start) & (row_i[lo:hi] < start + DT)
            kt_s[8 * g + h, pl.ds(0, 128 * n), :] = jnp.where(rm, kt[lo:hi], 0.0).astype(BF16)
            lm = (lane_i[:, lo:hi] >= start) & (lane_i[:, lo:hi] < start + DT)
            v_s[8 * g + h, :, pl.ds(0, 128 * n)] = jnp.where(lm, v_full[:, lo:hi], 0.0).astype(BF16)
    fetch["tmask"].wait()
    fetch["pbias"].wait()

    def one_copy(g, d):
        return remote(snd.at[g, d], rcv.at[g, lax.rem(c // (1 + 3 * g), 4)], one_s.at[g, d],
                      one_r.at[g, lax.rem(c // (1 + 3 * g), 4)], (r, (y * 4 + d) * (1 - g) + (d * 4 + x) * g))

    def attend(step, carry):
        g = lax.rem(step, 2)
        me = lax.rem(c // (1 + 3 * g), 4)
        d = lax.rem(me + 1 + step // 2, 4)
        blocks = [b * (4 - 3 * g) + d * (1 + 3 * g) for b in range(4)]
        rows = [pl.ds(pl.multiple_of(j * OWN, OWN), OWN) for j in blocks]
        live = tmask[...] == 1
        lane8 = lax.rem(iota((128, 128), 1), 8)
        parts = [jnp.zeros((128, 128), F32) for _ in range(3)]
        stat = jnp.zeros((128, 128), F32)
        for h in range(8):
            b0, n = SPANS[h]
            lanes = pl.ds(pl.multiple_of(g * G + 128 * b0, 128), 128 * n)
            qw = jnp.concatenate([q_s[rw, lanes] for rw in rows], axis=0)
            s = dot(qw, kt_s[g * 8 + h, pl.ds(0, 128 * n), :])
            s = s + jnp.concatenate([pbias[g * 8 + h, rw, :] for rw in rows], axis=0).astype(F32)
            s = jnp.where(live, s, MASKED)
            top = jnp.max(s, axis=-1, keepdims=True)
            e = jnp.exp(s - top)
            total = jnp.sum(e, axis=-1, keepdims=True)
            o = dot(e.astype(BF16), v_s[g * 8 + h, :, pl.ds(0, 128 * n)]) * (1.0 / total)
            for b in range(n):
                parts[b0 + b] = parts[b0 + b] + o[:, 128 * b : 128 * (b + 1)]
            stat = jnp.where(lane8 == h, top + jnp.log(total), stat)
        snd[g, d] = jnp.concatenate(parts + [split_lse(stat)], axis=1).astype(BF16)

        @pl.when(d != me)
        def _():
            one_copy(g, d).start()

        return carry

    lax.fori_loop(0, 8, attend, 0)

    mine = (x, y)

    def two_copy(g, d):
        dev = (r, d * 4 + x) if g == 0 else (r, y * 4 + d)
        me = mine[1 - g]
        return remote(snd2.at[g, d], rcv2.at[g, me], two_s.at[g, d], two_r.at[g, me], dev)

    for g in range(2):
        blocks = [snd[g, mine[g]]]
        for i in (1, 3, 2):
            d = lax.rem(mine[g] + i, 4)
            remote(snd.at[g, d], rcv.at[g, d], one_s.at[g, d], one_r.at[g, d], (r, near[g](i))).wait_recv()
            blocks.append(rcv[g, d])
        half_merged = merge(blocks, True)
        for d in range(4):
            snd2[g, d] = half_merged[OWN * d : OWN * (d + 1)]
        for i in (1, 3, 2):
            two_copy(g, lax.rem(mine[1 - g] + i, 4)).start()
    merged = []
    for g in range(2):
        blocks = [snd2[g, mine[1 - g]]]
        for i in (1, 3, 2):
            d = lax.rem(mine[1 - g] + i, 4)
            remote(snd2.at[g, d], rcv2.at[g, d], two_s.at[g, d], two_r.at[g, d], (r, near[1 - g](i))).wait_recv()
            blocks.append(rcv2[g, d])
        merged.append(merge(blocks, False))
    att = jnp.concatenate(merged, axis=1)

    for name in ("to", "rg", "ru", "rd", "back"):
        fetch[name].wait()
    gated = (att * gate_t).astype(BF16)
    t_att = (tmid[own_rows, :].astype(F32) + dot(gated, to[...])).astype(BF16)
    n_att = norm(t_att.astype(F32)).astype(BF16)
    up = dot(n_att, rg[...])
    hid = (up * sigmoid(up) * dot(n_att, ru[...])).astype(BF16)
    t_new = (t_att.astype(F32) + dot(hid, rd[...])).astype(BF16)
    g_new[...] = t_new

    def new_rows(half, s):
        return tokens_out.at[pl.ds(pl.multiple_of(s * OWN + 16 * half, 16), 16)]

    def new_copy(half, s, slot, dev, own):
        src = g_new.at[pl.ds(16 * half, 16)] if own else new_rows(half, s)
        return remote(src, new_rows(half, s), new_s.at[half, slot], new_r.at[half, s], (r, dev))

    for half in range(2):

        def first_new(s, slot, dev, arrives):
            if arrives is None:
                new_copy(half, s, slot, dev, True).start()

        hops(half, first_new)
    own_new = pltpu.make_async_copy(g_new, tokens_out.at[own_rows], own_sem.at[0])
    own_new.start()
    g_upd[c] = dot(t_new, back[...]).astype(BF16)

    def upd_copy(i):
        return remote(g_upd.at[c], g_upd.at[c], upd_s.at[col_peer(i)], upd_r.at[c], (r, col_peer(i)))

    for i in range(1, COLS):
        upd_copy(i).start()
    tok_t = jnp.broadcast_to((tk[c] - r * T).astype(F32), (128, A)).T
    lane_f = iota((A, 128), 1).astype(F32)
    pick = jnp.concatenate(
        [jnp.where(tok_t == lane_f + 128.0 * b, 1.0, 0.0).astype(BF16) for b in range(T // 128)], axis=1
    )
    for half in range(2):

        def onward_new(s, slot, dev, arrives):
            if arrives is None:
                return
            if arrives:
                new_copy(half, s, slot, dev, False).wait_recv()
            new_copy(half, s, slot, dev, False).start()

        hops(half, onward_new)

    for i in range(1, COLS):
        s = col_peer(i)
        remote(g_upd.at[s], g_upd.at[s], upd_s.at[s], upd_r.at[s], (r, s)).wait_recv()
    update = dot(pick, g_upd[...].reshape(T, 128))
    atoms_out[...] = (g_mid[c].astype(F32) + update).astype(BF16)

    for half in range(2):
        for i in (1, 3, 2):
            for j in range(4):
                s = y_peer(i) // 4 * 4 + j if half == 0 else j * 4 + lax.rem(x + i, 4)
                new_copy(half, s, 0, s, False).wait_recv()
    own_new.wait()
    for cp in halo:
        cp.wait_send()
    for i in range(1, COLS):
        tok_copy(i).wait_send()
        upd_copy(i).wait_send()
    for half in range(2):

        def sent(s, slot, dev, arrives):
            mid_copy(half, s, slot, dev).wait_send()
            new_copy(half, s, slot, dev, arrives is None).wait_send()

        hops(half, sent)
    for g in range(2):
        for i in (1, 3, 2):
            one_copy(g, lax.rem(mine[g] + i, 4)).wait_send()
            two_copy(g, lax.rem(mine[1 - g] + i, 4)).wait_send()

    @pl.when(is_src)
    def _():
        for n in range(PARTS):
            for j in (0, 1, 3):
                key_send(n, j).wait_send()

    @pl.when(on_core & (away != 0))
    def _():
        for n in range(PARTS):
            key_across(n).wait_send()

    @pl.when(relays)
    def _():
        for n in range(2):
            key_on(lax.rem(n + shift, PARTS)).wait_send()


def on_device(
    atoms, atom_bias, key_mask, atom_token, tokens, pair_bias, token_mask,
    atom_query, atom_keyval, atom_gate, atom_out, pool_weight,
    token_query, token_keyval, token_gate, token_out, trans_gate, trans_up, trans_down, back_weight,
):
    args = (
        atoms, atom_bias.reshape(A * HA, WK), key_mask, atom_token.reshape(1, A), tokens, pair_bias,
        token_mask.reshape(1, K), atom_query, atom_keyval, atom_gate, atom_out, pool_weight,
        token_query, token_keyval, token_gate, token_out, trans_gate, trans_up, trans_down, back_weight,
    )
    vmem = [pltpu.VMEM(a.shape, a.dtype) for a in args]
    vmem[0] = pltpu.VMEM((A + 2 * REACH, 128), BF16)
    vmem[3] = pltpu.VMEM((COLS, 1, A), jnp.int32)
    dma = pltpu.SemaphoreType.DMA
    scratch = vmem + [
        pltpu.VMEM((COLS, A, 128), BF16),
        pltpu.VMEM((COLS * A, C), BF16),
        pltpu.VMEM((T, C), F32),
        pltpu.VMEM((T, H), F32),
        pltpu.VMEM((T, C), BF16),
        pltpu.VMEM((T, C), BF16),
        pltpu.VMEM((K, C), BF16),
        pltpu.VMEM((T, C), BF16),
        pltpu.VMEM((16, 256, K), BF16),
        pltpu.VMEM((16, K, 256), BF16),
        pltpu.VMEM((2, 4, 4 * OWN, G + 128), BF16),
        pltpu.VMEM((2, 4, 4 * OWN, G + 128), BF16),
        pltpu.VMEM((2, 4, OWN, G + 128), BF16),
        pltpu.VMEM((2, 4, OWN, G + 128), BF16),
        pltpu.VMEM((OWN, C), BF16),
        pltpu.VMEM((COLS, OWN, 128), BF16),
        dma((len(args),)), dma((2,)), dma((2,)),
        dma((COLS,)), dma((COLS,)), dma((2, COLS)), dma((2, COLS)),
        dma((PARTS, 4)), dma((PARTS,)),
        dma((2, 4)), dma((2, 4)), dma((2, 4)), dma((2, 4)),
        dma((COLS,)), dma((COLS,)), dma((2, COLS)), dma((2, COLS)), dma((1,)),
    ]
    return pl.pallas_call(
        kernel,
        out_shape=(jax.ShapeDtypeStruct((A, 128), BF16), jax.ShapeDtypeStruct((T, C), BF16)),
        in_specs=[pl.BlockSpec(memory_space=pl.ANY)] * len(args),
        out_specs=(pl.BlockSpec(memory_space=pltpu.VMEM), pl.BlockSpec(memory_space=pl.ANY)),
        scratch_shapes=scratch,
        compiler_params=pltpu.CompilerParams(
            collective_id=0, has_side_effects=True, vmem_limit_bytes=60 * 1024 * 1024
        ),
        name="block",
    )(*args)


def solution(mesh):
    both = ("row", "col")
    in_specs = (
        P(both, None), P(both, None, None), P(both, None), P(both), P("row", None), P(None, "row", "col"), P("col"),
    ) + (P(),) * 13
    out_specs = (P(both, None), P("row", None))
    return jax.shard_map(on_device, mesh=mesh, in_specs=in_specs, out_specs=out_specs, check_vma=False)
```

```python
import functools

import jax
import jax.numpy as jnp
from jax import lax
from jax.experimental import pallas as pl
from jax.experimental.pallas import tpu as pltpu
from jax.sharding import PartitionSpec as P

F32 = jnp.float32
BF16 = jnp.bfloat16
MESH = pl.DeviceIdType.MESH
ROWS, COLS = 8, 16
EPSILON = 1e-05
MASKED = -1000000000.0
HA, DA, WQ, WK = 4, 32, 32, 128
DT = 48
REACH = 48
A = 256
T = 512
K = 256
C = 768
G = 384
OWN = 32
H = 128
TOTAL_ATOMS = 32768


def dot(a, b):
    return jnp.dot(a, b, preferred_element_type=F32)


def norm(x):
    mean = jnp.mean(x, axis=-1, keepdims=True)
    d = x - mean
    var = jnp.mean(d * d, axis=-1, keepdims=True)
    return d * lax.rsqrt(var + EPSILON)


def sigmoid(x):
    return 1.0 / (1.0 + jnp.exp(-x))


def iota(shape, dim):
    return lax.broadcasted_iota(jnp.int32, shape, dim)


IN_NAMES = (
    "atoms", "abias", "kmask", "atok", "tokens", "pbias", "tmask", "aq", "akv", "ag", "ao", "pool",
    "tq", "tkv", "tg", "to", "rg", "ru", "rd",
)
EARLY = ("atoms", "akv", "aq", "ag", "kmask", "abias", "ao", "atok", "pool")
LATE = ("tokens", "tg", "tq", "tkv", "tmask", "pbias", "to", "rg", "ru", "rd")
SPANS = tuple(((DT * h) // 128, (DT * h + DT - 1) // 128 - (DT * h) // 128 + 1) for h in range(8))


def split_lse(stat):
    high = stat.astype(BF16).astype(F32)
    rest = stat - high
    middle = rest.astype(BF16).astype(F32)
    third = iota(stat.shape, 1) // 8
    return jnp.where(third == 0, high, jnp.where(third == 1, middle, rest - middle))


def join_lse():
    l_r, l_c = iota((128, 128), 0), iota((128, 128), 1)
    return jnp.where((l_r < 24) & (lax.rem(l_r, 8) == lax.rem(l_c, 8)), 1.0, 0.0).astype(BF16)


def merge(values, lse, want_lse):
    s_r, s_c = iota((128, G), 0), iota((128, G), 1)
    spread = jnp.where((s_r < 16) & (lax.rem(s_r, 8) == s_c // DT), 1.0, 0.0).astype(BF16)
    top = lse[0]
    for l in lse[1:]:
        top = jnp.maximum(top, l)
    wgt = [jnp.exp(l - top) for l in lse]
    total = wgt[0]
    for w in wgt[1:]:
        total = total + w
    inv = 1.0 / total
    first = iota(top.shape, 1) < 8
    out = None
    for w, v in zip(wgt, values):
        w = w * inv
        high = w.astype(BF16).astype(F32)
        term = dot(jnp.where(first, high, w - high).astype(BF16), spread) * v.astype(F32)
        out = term if out is None else out + term
    if want_lse:
        return jnp.concatenate([out, split_lse(top + jnp.log(total))], axis=1).astype(BF16)
    return out


def kernel(*refs):
    n_in = len(IN_NAMES)
    hbm = dict(zip(IN_NAMES, refs[:n_in]))
    mid_out, tokens_out = refs[n_in : n_in + 2]
    (
        ext, abias, kmask, tk, tokens, pbias, tmask, aq, akv, ag, ao, pool, tq, tkv, tg, to, rg, ru, rd,
        g_mid, feats, acc, selsum, tmid, tnorm, knorm, q_s, kt_s, v_s, snd, rcv, snd2, rcv2, g_new,
        in_sem, halo_s, halo_r, tok_s, tok_r, mid_s, mid_r, key_s, key_r,
        one_s, one_r, two_s, two_r, new_s, new_r, own_sem,
    ) = refs[n_in + 2 :]

    r = lax.axis_index("row")
    c = lax.axis_index("col")
    y, x = c // 4, lax.rem(c, 4)
    z, core = r // 2, lax.rem(r, 2)
    lin = r * COLS + c
    nxt = lax.rem(lin + 1, ROWS * COLS)
    prv = lax.rem(lin + ROWS * COLS - 1, ROWS * COLS)
    nxt_id = (nxt // COLS, lax.rem(nxt, COLS))
    prv_id = (prv // COLS, lax.rem(prv, COLS))
    sibling = (z * 2 + 1 - core, c)

    def remote(src, dst, ss, rs, dev):
        return pltpu.make_async_remote_copy(
            src_ref=src, dst_ref=dst, send_sem=ss, recv_sem=rs, device_id=dev, device_id_type=MESH
        )

    def col_peer(i):
        return lax.rem(c + i, COLS)

    def x_peer(i):
        return y * 4 + lax.rem(x + i, 4)

    def y_peer(i):
        return lax.rem(y + i, 4) * 4 + x

    near = (x_peer, y_peer)

    bar = pltpu.get_barrier_semaphore()
    for dev in (nxt_id, prv_id, sibling, (lax.rem(z + 1, 4) * 2 + core, c), (lax.rem(z + 3, 4) * 2 + core, c)):
        pl.semaphore_signal(bar, inc=1, device_id=dev, device_id_type=MESH)
    for i in range(1, COLS):
        pl.semaphore_signal(bar, inc=1, device_id=(r, col_peer(i)), device_id_type=MESH)

    fetch = {}
    vm = dict(
        atoms=ext.at[pl.ds(REACH, A)], abias=abias, kmask=kmask, atok=tk.at[c], tokens=tokens, pbias=pbias, tmask=tmask,
        aq=aq, akv=akv, ag=ag, ao=ao, pool=pool, tq=tq, tkv=tkv, tg=tg, to=to, rg=rg, ru=ru, rd=rd,
    )
    for i, name in enumerate(EARLY + LATE):
        fetch[name] = pltpu.make_async_copy(hbm[name], vm[name], in_sem.at[i])
    for name in EARLY:
        fetch[name].start()

    for name in ("atoms", "akv", "aq", "ag"):
        fetch[name].wait()
    own_f = ext[pl.ds(REACH, A), :].astype(F32)
    own_n = norm(own_f).astype(BF16)
    q_a = dot(own_n, aq[...]).astype(BF16)
    gate_a = sigmoid(dot(own_n, ag[...]))
    kv_own = dot(own_n, akv[...]).astype(BF16)
    fetch["kmask"].wait()
    fetch["abias"].wait()
    p_r = iota((HA * WQ, HA * WQ), 0)
    p_c = iota((HA * WQ, HA * WQ), 1)
    perm = (p_c == lax.rem(p_r, WQ) * HA + p_r // WQ).astype(F32).astype(BF16)
    bias_w = [dot(perm, abias[pl.ds(HA * WQ * w, HA * WQ), :]) for w in range(A // WQ)]
    lane = iota((1, WK), 1)
    head_f = [jnp.where((lane // DA) == h, 1.0, 0.0).astype(F32) for h in range(HA)]
    head_b = [f.astype(BF16) for f in head_f]

    def window(w, kv):
        q_w = q_a[WQ * w : WQ * (w + 1)]
        q_bd = jnp.concatenate([q_w * head_b[h] for h in range(HA)], axis=0)
        s = lax.dot_general(q_bd, kv[:, :WK], (((1,), (1,)), ((), ())), preferred_element_type=F32)
        s = s * (DA**-0.5) + bias_w[w]
        pos = lin * A + WQ * w + lane - REACH
        valid = (kmask[pl.ds(w, 1), :] == 1) & (pos >= 0) & (pos < TOTAL_ATOMS)
        s = jnp.where(valid, s, MASKED)
        e = jnp.exp(s - jnp.max(s, axis=-1, keepdims=True))
        t = jnp.sum(e, axis=-1, keepdims=True)
        o = dot(e.astype(BF16), kv[:, WK:]) / t
        return sum(o[WQ * h : WQ * (h + 1)] * head_f[h] for h in range(HA))

    def mid_of(first, attended):
        rows = slice(first, first + WQ * len(attended))
        gated = (jnp.concatenate(attended, axis=0) * gate_a[rows]).astype(BF16)
        return (own_f[rows] + dot(gated, ao[...])).astype(BF16)

    fetch["ao"].wait()
    g_mid[c, 0:H, :] = mid_of(64, [window(w, kv_own[WQ * w - REACH : WQ * w - REACH + WK]) for w in (2, 3, 4, 5)])
    pl.semaphore_wait(bar, 5 + COLS - 1)

    halo = [
        remote(hbm["atoms"].at[pl.ds(A - REACH, REACH)], ext.at[pl.ds(0, REACH)], halo_s.at[0], halo_r.at[0], nxt_id),
        remote(hbm["atoms"].at[pl.ds(0, REACH)], ext.at[pl.ds(REACH + A, REACH)], halo_s.at[1], halo_r.at[1], prv_id),
    ]
    for cp in halo:
        cp.start()

    def tok_copy(i):
        return remote(hbm["atok"], tk.at[c], tok_s.at[col_peer(i)], tok_r.at[c], (r, col_peer(i)))

    def mid_at(half, s):
        return g_mid.at[s, pl.ds(H * half, H)]

    def mid_copy(half, s, slot, dev):
        return remote(mid_at(half, s), mid_at(half, s), mid_s.at[half, slot], mid_r.at[half, s], (r, dev))

    def hops(half, send):
        for i in (1, 3, 2):
            send(c, i - 1, near[half](i), None)
        for i in (1, 3, 2):
            send(c, i + 2, near[1 - half](i), None)
        for far in (False, True):
            for k, j in enumerate((1, 3, 2)):
                s = near[half](j)
                for i in (2,) if far else (1, 3):
                    send(s, 3 * k + i + 5, near[1 - half](i), i == 1)

    def first(half):
        def send(s, slot, dev, arrives):
            if arrives is None:
                mid_copy(half, s, slot, dev).start()

        hops(half, send)

    first(0)
    for i in range(1, COLS):
        tok_copy(i).start()
    for name in LATE:
        fetch[name].start()
    edges = []
    for side in range(2):
        halo[side].wait_recv()
        edge = norm(ext[pl.ds((REACH + A) * side, REACH), :].astype(F32)).astype(BF16)
        inside = jnp.where(lin == (ROWS * COLS - 1) * side, 0.0, 1.0).astype(F32)
        edges.append((dot(edge, akv[...]) * inside).astype(BF16))
    near_by = jnp.concatenate([kv_own[6 * WQ - REACH :], edges[1]], axis=0)
    g_mid[c, H : H + 64, :] = mid_of(192, [window(6, near_by[:WK]), window(7, near_by[WQ : WQ + WK])])
    near_by = jnp.concatenate([edges[0], kv_own[: WK - WQ + 16]], axis=0)
    g_mid[c, H + 64 :, :] = mid_of(0, [window(0, near_by[:WK]), window(1, near_by[WQ : WQ + WK])])
    first(1)
    mid_out_copies = [
        pltpu.make_async_copy(g_mid.at[c, pl.ds(a, n)], mid_out.at[pl.ds(b, n)], own_sem.at[i])
        for i, (a, b, n) in enumerate(((0, 64, H), (H, 192, 64), (H + 64, 0, 64)))
    ]
    for cp in mid_out_copies:
        cp.start()

    fetch["pool"].wait()
    fetch["atok"].wait()
    for i in range(1, COLS):
        s = col_peer(i)
        remote(hbm["atok"], tk.at[s], tok_s.at[s], tok_r.at[s], (r, s)).wait_recv()
    for half in range(2):

        def onward(s, slot, dev, arrives):
            if arrives is None:
                return
            if arrives:
                mid_copy(half, s, slot, dev).wait_recv()
            mid_copy(half, s, slot, dev).start()

        hops(half, onward)

    key_off = lax.rem(c, 2) * K

    def step_blocks(step):
        o = lax.rem(step * (step + 1) // 2, 4)
        a = [(lax.rem(y + o, 4) * 4 + b, 0) for b in range(4)]
        return a + [(b * 4 + lax.rem(x + o, 4), 1) for b in range(4)]

    def selector(step, off):
        base = r * T + off
        at = iota((K, H), 0)
        sel = []
        for s, half in step_blocks(step):
            turned = pltpu.roll(jnp.broadcast_to(tk[s] - base, (8, A)), 64, 1)
            sel.append(jnp.where(at == turned[0:1, H * (1 - half) : H * (2 - half)], 1.0, 0.0).astype(F32))
        return sel

    def pool_into(off, step, sel):
        rows = pl.ds(pl.multiple_of(off, K), K)
        count = sel[0]
        for m in sel[1:]:
            count = count + m
        selsum[rows, :] += count
        sel = jnp.concatenate([m.astype(BF16) for m in sel], axis=1)
        acc[rows, :] += dot(sel, feats[pl.ds(pl.multiple_of(step * 1024, 1024), 1024), :])

    acc[...] = jnp.zeros(acc.shape, F32)
    selsum[...] = jnp.zeros(selsum.shape, F32)

    def pool_step(step, carry):
        @pl.when(step > 0)
        def _():
            for s, half in step_blocks(step):
                mid_copy(half, s, 0, s).wait_recv()

        for n, (s, half) in enumerate(step_blocks(step)):
            f = jnp.maximum(dot(g_mid[s, pl.ds(H * half, H), :], pool[...]), 0.0).astype(BF16)
            feats[pl.ds(pl.multiple_of(step * 1024 + H * n, H), H), :] = f
        pool_into(key_off, step, selector(step, key_off))
        return carry

    lax.fori_loop(0, 4, pool_step, 0)
    fetch["tokens"].wait()
    ones = jnp.ones((H, 128), BF16)

    def finish_chunk(first):
        rows = pl.ds(pl.multiple_of(first, 128), 128)
        inv = 1.0 / dot(selsum[rows, :].astype(BF16), ones)
        inv = jnp.concatenate([inv] * (C // 128), axis=1)
        m = (tokens[rows, :].astype(F32) + acc[rows, :] * inv).astype(BF16)
        tmid[rows, :] = m
        tnorm[rows, :] = norm(m.astype(F32)).astype(BF16)

    z0, core0 = (c // 2) // 2, lax.rem(c // 2, 2)
    away = lax.rem(z - z0 + 4, 4)
    on_core = core == core0
    is_src = on_core & (away == 0)
    is_sib = jnp.logical_not(on_core) & (away == 0)
    odd = jnp.where(on_core, 0, 1)
    swap = jnp.where(away == 3, 1, 0)
    up, down = (lax.rem(z + 1, 4) * 2 + core, c), (lax.rem(z + 3, 4) * 2 + core, c)
    onward_id = (lax.rem(z + away, 4) * 2 + core, c)

    def key_copy(q, slot, dev):
        rows = knorm.at[pl.ds(pl.multiple_of(q * OWN, OWN), OWN)]
        return remote(rows, rows, key_s.at[q, slot], key_r.at[q], dev)

    def chip_part(n):
        return 2 * lax.rem(n + 2 * swap, 4) + odd

    for pair in range(2):
        finish_chunk(key_off + 128 * pair)

        @pl.when(is_src)
        def _():
            rows = pl.ds(pl.multiple_of(key_off + 128 * pair, 128), 128)
            knorm[pl.ds(128 * pair, 128), :] = tnorm[rows, :]
            q = 4 * pair
            for p in (q + 1, q + 3):
                key_copy(p, 2, sibling).start()
            for p in (q, q + 2):
                key_copy(p, 0, up).start()
            if pair == 1:
                for p in (4, 6, 0, 2):
                    key_copy(p, 1, down).start()
            for p in (q, q + 2):
                key_copy(p, 2, sibling).start()

    @pl.when(is_sib)
    def _():
        for p in (1, 3, 5, 7):
            key_copy(p, 0, up).wait_recv()
            key_copy(p, 0, up).start()
            if p > 4:
                key_copy(p, 1, down).start()
        for p in (1, 3):
            key_copy(p, 1, down).start()

    other_off = K - key_off

    def other_step(step, carry):
        pool_into(other_off, step, selector(step, other_off))

        return carry

    lax.fori_loop(0, 4, other_step, 0)
    own_rows = pl.ds(pl.multiple_of(c * OWN, OWN), OWN)
    for n in range(4):

        @pl.when(away != 0)
        def _():
            key_copy(chip_part(n), 2, sibling).wait_recv()
            key_copy(chip_part(n), 2, sibling).start()

        if n < 2:

            @pl.when((away == 1) | (away == 3))
            def _():
                key_copy(chip_part(n), 0, onward_id).start()

        if n < 2:
            finish_chunk(other_off + 128 * n)
        else:
            if n == 2:
                fetch["tq"].wait()
                fetch["tg"].wait()
            for i in (2 * n - 4, 2 * n - 3):
                q_s[pl.ds(128 * i, 128), :] = dot(tnorm[pl.ds(128 * i, 128), :], tq[...]).astype(BF16)
    gate_t = sigmoid(dot(tnorm[own_rows, :], tg[...]))

    @pl.when(jnp.logical_not(is_src))
    def _():
        for n in range(4):
            q = 2 * n + 1 - odd
            key_copy(q, 2, sibling).wait_recv()

    fetch["tkv"].wait()
    kt = (dot(knorm[...], tkv[:, :C]) * (DT**-0.5)).T
    row_i = iota((C, 1), 0)
    v_full = dot(knorm[...], tkv[:, C:])
    lane_i = iota((1, C), 1)
    for g in range(2):
        for h in range(8):
            b0, n = SPANS[h]
            lo, hi = G * g + 128 * b0, G * g + 128 * (b0 + n)
            start = G * g + DT * h
            rm = (row_i[lo:hi] >= start) & (row_i[lo:hi] < start + DT)
            kt_s[8 * g + h, pl.ds(0, 128 * n), :] = jnp.where(rm, kt[lo:hi], 0.0).astype(BF16)
            lm = (lane_i[:, lo:hi] >= start) & (lane_i[:, lo:hi] < start + DT)
            v_s[8 * g + h, :, pl.ds(0, 128 * n)] = jnp.where(lm, v_full[:, lo:hi], 0.0).astype(BF16)
    fetch["tmask"].wait()
    fetch["pbias"].wait()

    def one_copy(g, d):
        return remote(snd.at[g, d], rcv.at[g, lax.rem(c // (1 + 3 * g), 4)], one_s.at[g, d],
                      one_r.at[g, lax.rem(c // (1 + 3 * g), 4)], (r, (y * 4 + d) * (1 - g) + (d * 4 + x) * g))

    def attend(offsets, g, carry):
        me = lax.rem(c // (1 + 3 * g), 4)
        dests = [lax.rem(me + o, 4) for o in offsets]
        size = 128 * len(dests)
        rows = [
            pl.ds(pl.multiple_of((b * (4 - 3 * g) + d * (1 + 3 * g)) * OWN, OWN), OWN) for d in dests for b in range(4)
        ]
        live = tmask[...] == 1
        lane8 = lax.rem(iota((size, 128), 1), 8)
        parts = [None] * 3
        stat = jnp.zeros((size, 128), F32)
        for h in range(8):
            b0, n = SPANS[h]
            lanes = pl.ds(pl.multiple_of(g * G + 128 * b0, 128), 128 * n)
            qw = jnp.concatenate([q_s[rw, lanes] for rw in rows], axis=0)
            s = dot(qw, kt_s[g * 8 + h, pl.ds(0, 128 * n), :])
            s = s + jnp.concatenate([pbias[g * 8 + h, rw, :] for rw in rows], axis=0).astype(F32)
            s = jnp.where(live, s, MASKED)
            top = jnp.max(s, axis=-1, keepdims=True)
            e = jnp.exp(s - top)
            total = jnp.sum(e, axis=-1, keepdims=True)
            o = dot(e.astype(BF16), v_s[g * 8 + h, :, pl.ds(0, 128 * n)]) * (1.0 / total)
            for b in range(n):
                ob = o[:, 128 * b : 128 * (b + 1)]
                parts[b0 + b] = ob if parts[b0 + b] is None else parts[b0 + b] + ob
            stat = jnp.where(lane8 == h, top + jnp.log(total), stat)
        stat = split_lse(stat)
        for n, d in enumerate(dests):
            for b in range(3):
                snd[g, d, pl.ds(128 * b, 128), :] = parts[b][128 * n : 128 * (n + 1)].astype(BF16)
            snd[g, d, pl.ds(G, 32), :] = stat[128 * n : 128 * (n + 1)].T[:32].astype(BF16)

            if offsets[n] != 0:
                one_copy(g, d).start()

        return carry

    for offsets in ((2,), (1, 3), (0,)):
        lax.fori_loop(0, 2, functools.partial(attend, offsets), 0)

    mine = (x, y)
    join = join_lse()

    def two_copy(g, d):
        dev = (r, d * 4 + x) if g == 0 else (r, y * 4 + d)
        me = mine[1 - g]
        return remote(snd2.at[g, d], rcv2.at[g, me], two_s.at[g, d], two_r.at[g, me], dev)

    for g in range(2):
        blocks = [snd[g, mine[g]]]
        for i in (2, 3, 1):
            d = lax.rem(mine[g] + i, 4)
            remote(snd.at[g, d], rcv.at[g, d], one_s.at[g, d], one_r.at[g, d], (r, near[g](i))).wait_recv()
            blocks.append(rcv[g, d])
        values = [jnp.concatenate([b[128 * k : 128 * (k + 1)] for k in range(3)], axis=1) for b in blocks]
        lse = [
            lax.dot_general(b[G:], join[:32], (((0,), (0,)), ((), ())), preferred_element_type=F32) for b in blocks
        ]
        half_merged = merge(values, lse, True)
        for d in range(4):
            snd2[g, d] = half_merged[OWN * d : OWN * (d + 1)]
        for i in (1, 3, 2):
            two_copy(g, lax.rem(mine[1 - g] + i, 4)).start()
    merged = []
    for g in range(2):
        blocks = [snd2[g, mine[1 - g]]]
        for i in (1, 3, 2):
            d = lax.rem(mine[1 - g] + i, 4)
            remote(snd2.at[g, d], rcv2.at[g, d], two_s.at[g, d], two_r.at[g, d], (r, near[1 - g](i))).wait_recv()
            blocks.append(rcv2[g, d])
        merged.append(merge([b[:, :G] for b in blocks], [dot(b[:, G:], join) for b in blocks], False))
    att = jnp.concatenate(merged, axis=1)

    for name in ("to", "rg", "ru", "rd"):
        fetch[name].wait()
    gated = (att * gate_t).astype(BF16)
    t_att = (tmid[own_rows, :].astype(F32) + dot(gated, to[...])).astype(BF16)
    n_att = norm(t_att.astype(F32)).astype(BF16)
    up = dot(n_att, rg[...])
    hid = (up * sigmoid(up) * dot(n_att, ru[...])).astype(BF16)
    t_new = (t_att.astype(F32) + dot(hid, rd[...])).astype(BF16)
    g_new[own_rows, :] = t_new

    def rows_of(half, s):
        return pl.ds(pl.multiple_of(s * OWN + 16 * half, 16), 16)

    def new_copy(half, s, slot, dev):
        dst = g_new if slot < 3 else tokens_out
        return remote(
            g_new.at[rows_of(half, s)], dst.at[rows_of(half, s)], new_s.at[half, slot], new_r.at[half, s], (r, dev)
        )

    out_copies = [pltpu.make_async_copy(g_new.at[own_rows], tokens_out.at[own_rows], own_sem.at[3])]
    for half in range(2):

        def first_new(s, slot, dev, arrives):
            if arrives is None:
                new_copy(half, s, slot, dev).start()

        hops(half, first_new)
    out_copies[0].start()
    for half in range(2):
        for k, i in enumerate((1, 3, 2)):
            rows = rows_of(half, near[half](i))
            out_copies.append(pltpu.make_async_copy(g_new.at[rows], tokens_out.at[rows], own_sem.at[4 + 3 * half + k]))

    for half in range(2):

        def onward_new(s, slot, dev, arrives):
            if arrives is None:
                return
            if arrives:
                new_copy(half, s, 0, dev).wait_recv()
            new_copy(half, s, slot, dev).start()

        hops(half, onward_new)
    for cp in out_copies[1:]:
        cp.start()

    for half in range(2):
        for i in (1, 3, 2):
            for j in range(4):
                s = y_peer(i) // 4 * 4 + j if half == 0 else j * 4 + lax.rem(x + i, 4)
                new_copy(half, s, 3, s).wait_recv()
    for cp in mid_out_copies + out_copies:
        cp.wait()
    for cp in halo:
        cp.wait_send()
    for i in range(1, COLS):
        tok_copy(i).wait_send()
    for half in range(2):

        def sent(s, slot, dev, arrives):
            mid_copy(half, s, slot, dev).wait_send()
            new_copy(half, s, slot, dev).wait_send()

        hops(half, sent)
    for g in range(2):
        for i in (1, 3, 2):
            one_copy(g, lax.rem(mine[g] + i, 4)).wait_send()
            two_copy(g, lax.rem(mine[1 - g] + i, 4)).wait_send()

    @pl.when(is_src)
    def _():
        for q in range(8):
            key_copy(q, 2, sibling).wait_send()
            if q % 2 == 0:
                key_copy(q, 0, up).wait_send()
                key_copy(q, 1, down).wait_send()

    @pl.when(is_sib)
    def _():
        for q in (1, 3, 5, 7):
            key_copy(q, 0, up).wait_send()
            key_copy(q, 1, down).wait_send()

    @pl.when(away != 0)
    def _():
        for n in range(4):
            key_copy(chip_part(n), 2, sibling).wait_send()

    @pl.when((away == 1) | (away == 3))
    def _():
        for n in (0, 1):
            key_copy(chip_part(n), 0, onward_id).wait_send()


def to_atoms(mid, new, back, atok, atoms_out, tokens_out, mid_v, new_v, back_v, atok_v, in_sem, out_sem):
    n = 4
    rows = [pl.ds(i * (T // n), T // n) for i in range(n)]
    ins = [pltpu.make_async_copy(new.at[w], new_v.at[w], in_sem.at[i]) for i, w in enumerate(rows)]
    small = [
        pltpu.make_async_copy(a, b, in_sem.at[n + i])
        for i, (a, b) in enumerate(((atok, atok_v), (back, back_v), (mid, mid_v)))
    ]
    outs = [pltpu.make_async_copy(new_v.at[w], tokens_out.at[w], out_sem.at[i]) for i, w in enumerate(rows)]
    for cp in ins[:1] + small + ins[1:]:
        cp.start()
    first = lax.axis_index("row") * T
    lane = iota((A, 128), 1).astype(F32)
    ins[0].wait()
    outs[0].start()
    for cp in small:
        cp.wait()
    tok_t = jnp.broadcast_to((atok_v[...] - first).astype(F32), (128, A)).T
    update = None
    for i, w in enumerate(rows):
        if i > 0:
            ins[i].wait()
            outs[i].start()
        pick = jnp.where(tok_t == lane + float(T // n * i), 1.0, 0.0).astype(BF16)
        term = dot(pick, dot(new_v[w, :], back_v[...]).astype(BF16))
        update = term if update is None else update + term
    mid_v[...] = (mid_v[...].astype(F32) + update).astype(BF16)
    last = pltpu.make_async_copy(mid_v, atoms_out, out_sem.at[n])
    last.start()
    for cp in outs + [last]:
        cp.wait()


def on_device(
    atoms, atom_bias, key_mask, atom_token, tokens, pair_bias, token_mask,
    atom_query, atom_keyval, atom_gate, atom_out, pool_weight,
    token_query, token_keyval, token_gate, token_out, trans_gate, trans_up, trans_down, back_weight,
):
    atok = atom_token.reshape(1, A)
    args = (
        atoms, atom_bias.reshape(A * HA, WK), key_mask, atok, tokens, pair_bias,
        token_mask.reshape(1, K), atom_query, atom_keyval, atom_gate, atom_out, pool_weight,
        token_query, token_keyval, token_gate, token_out, trans_gate, trans_up, trans_down,
    )
    vmem = [pltpu.VMEM(a.shape, a.dtype) for a in args]
    vmem[0] = pltpu.VMEM((A + 2 * REACH, 128), BF16)
    vmem[3] = pltpu.VMEM((COLS, 1, A), jnp.int32)
    dma = pltpu.SemaphoreType.DMA
    scratch = vmem + [
        pltpu.VMEM((COLS, A, 128), BF16),
        pltpu.VMEM((COLS * A, C), BF16),
        pltpu.VMEM((T, C), F32),
        pltpu.VMEM((T, H), F32),
        pltpu.VMEM((T, C), BF16),
        pltpu.VMEM((T, C), BF16),
        pltpu.VMEM((K, C), BF16),
        pltpu.VMEM((T, C), BF16),
        pltpu.VMEM((16, 256, K), BF16),
        pltpu.VMEM((16, K, 256), BF16),
        pltpu.VMEM((2, 4, G + 32, 128), BF16),
        pltpu.VMEM((2, 4, G + 32, 128), BF16),
        pltpu.VMEM((2, 4, OWN, G + 128), BF16),
        pltpu.VMEM((2, 4, OWN, G + 128), BF16),
        pltpu.VMEM((T, C), BF16),
        dma((len(args),)), dma((2,)), dma((2,)),
        dma((COLS,)), dma((COLS,)), dma((2, COLS)), dma((2, COLS)),
        dma((8, 3)), dma((8,)),
        dma((2, 4)), dma((2, 4)), dma((2, 4)), dma((2, 4)),
        dma((2, COLS)), dma((2, COLS)), dma((10,)),
    ]
    mid, new = pl.pallas_call(
        kernel,
        out_shape=(jax.ShapeDtypeStruct((A, 128), BF16), jax.ShapeDtypeStruct((T, C), BF16)),
        in_specs=[pl.BlockSpec(memory_space=pl.ANY)] * len(args),
        out_specs=(pl.BlockSpec(memory_space=pl.ANY),) * 2,
        scratch_shapes=scratch,
        compiler_params=pltpu.CompilerParams(
            collective_id=0, has_side_effects=True, vmem_limit_bytes=60 * 1024 * 1024
        ),
        name="block",
    )(*args)
    hbm = pl.BlockSpec(memory_space=pl.ANY)
    return pl.pallas_call(
        to_atoms,
        out_shape=(jax.ShapeDtypeStruct((A, 128), BF16), jax.ShapeDtypeStruct((T, C), BF16)),
        in_specs=[hbm] * 4,
        out_specs=(hbm, hbm),
        scratch_shapes=[
            pltpu.VMEM((A, 128), BF16), pltpu.VMEM((T, C), BF16), pltpu.VMEM((C, 128), BF16), pltpu.VMEM((1, A), jnp.int32),
            dma((7,)), dma((5,)),
        ],
        compiler_params=pltpu.CompilerParams(vmem_limit_bytes=60 * 1024 * 1024),
        name="to_atoms",
    )(mid, new, back_weight, atok)


def solution(mesh):
    both = ("row", "col")
    in_specs = (
        P(both, None), P(both, None, None), P(both, None), P(both), P("row", None), P(None, "row", "col"), P("col"),
    ) + (P(),) * 13
    out_specs = (P(both, None), P("row", None))
    return jax.shard_map(on_device, mesh=mesh, in_specs=in_specs, out_specs=out_specs, check_vma=False)
```

```python
import functools

import jax
import jax.numpy as jnp
from jax import lax
from jax.experimental import pallas as pl
from jax.experimental.pallas import tpu as pltpu
from jax.sharding import PartitionSpec as P

F32 = jnp.float32
BF16 = jnp.bfloat16
MESH = pl.DeviceIdType.MESH
ROWS, COLS = 8, 16
EPSILON = 1e-05
MASKED = -1000000000.0
HA, DA, WQ, WK = 4, 32, 32, 128
DT = 48
REACH = 48
A = 256
T = 512
HEAD = 144
K = 256
C = 768
G = 384
OWN = 32
H = 128
TOTAL_ATOMS = 32768


def dot(a, b):
    return jnp.dot(a, b, preferred_element_type=F32)


def norm(x):
    mean = jnp.mean(x, axis=-1, keepdims=True)
    d = x - mean
    var = jnp.mean(d * d, axis=-1, keepdims=True)
    return d * lax.rsqrt(var + EPSILON)


def sigmoid(x):
    return 1.0 / (1.0 + jnp.exp(-x))


def iota(shape, dim):
    return lax.broadcasted_iota(jnp.int32, shape, dim)


IN_NAMES = (
    "atoms", "abias", "kmask", "atok", "tokens", "pbias", "tmask", "aq", "akv", "ag", "ao", "pool",
    "tq", "tkv", "tg", "to", "rg", "ru", "rd",
)
EARLY = ("atoms", "akv", "aq", "ag", "kmask", "abias", "ao", "atok", "pool")
LATE = ("tokens", "tg", "tq", "tkv", "tmask", "pbias", "to", "rg", "ru", "rd")
SPANS = tuple(((DT * h) // 128, (DT * h + DT - 1) // 128 - (DT * h) // 128 + 1) for h in range(8))


def split_lse(stat):
    high = stat.astype(BF16).astype(F32)
    rest = stat - high
    middle = rest.astype(BF16).astype(F32)
    third = iota(stat.shape, 1) // 8
    return jnp.where(third == 0, high, jnp.where(third == 1, middle, rest - middle))


def join_lse():
    l_r, l_c = iota((128, 128), 0), iota((128, 128), 1)
    return jnp.where((l_r < 24) & (lax.rem(l_r, 8) == lax.rem(l_c, 8)), 1.0, 0.0).astype(BF16)


def merge(values, lse, want_lse):
    s_r, s_c = iota((128, G), 0), iota((128, G), 1)
    spread = jnp.where((s_r < 16) & (lax.rem(s_r, 8) == s_c // DT), 1.0, 0.0).astype(BF16)
    top = lse[0]
    for l in lse[1:]:
        top = jnp.maximum(top, l)
    wgt = [jnp.exp(l - top) for l in lse]
    total = wgt[0]
    for w in wgt[1:]:
        total = total + w
    inv = 1.0 / total
    first = iota(top.shape, 1) < 8
    out = None
    for w, v in zip(wgt, values):
        w = w * inv
        high = w.astype(BF16).astype(F32)
        term = dot(jnp.where(first, high, w - high).astype(BF16), spread) * v.astype(F32)
        out = term if out is None else out + term
    if want_lse:
        return jnp.concatenate([out, split_lse(top + jnp.log(total))], axis=1).astype(BF16)
    return out


def kernel(*refs):
    n_in = len(IN_NAMES)
    hbm = dict(zip(IN_NAMES, refs[:n_in]))
    mid_out, tokens_out = refs[n_in : n_in + 2]
    (
        ext, abias, kmask, tk, tokens, pbias, tmask, aq, akv, ag, ao, pool, tq, tkv, tg, to, rg, ru, rd,
        g_mid, feats, acc, selsum, tmid, tnorm, knorm, q_s, kt_s, v_s, snd, rcv, snd2, rcv2, g_new,
        in_sem, halo_s, halo_r, mid_s, mid_r, key_s, key_r,
        one_s, one_r, two_s, two_r, new_s, new_r, own_sem,
    ) = refs[n_in + 2 :]

    r = lax.axis_index("row")
    c = lax.axis_index("col")
    y, x = c // 4, lax.rem(c, 4)
    z, core = r // 2, lax.rem(r, 2)
    lin = r * COLS + c
    nxt = lax.rem(lin + 1, ROWS * COLS)
    prv = lax.rem(lin + ROWS * COLS - 1, ROWS * COLS)
    nxt_id = (nxt // COLS, lax.rem(nxt, COLS))
    prv_id = (prv // COLS, lax.rem(prv, COLS))
    sibling = (z * 2 + 1 - core, c)

    def remote(src, dst, ss, rs, dev):
        return pltpu.make_async_remote_copy(
            src_ref=src, dst_ref=dst, send_sem=ss, recv_sem=rs, device_id=dev, device_id_type=MESH
        )

    def x_peer(i):
        return y * 4 + lax.rem(x + i, 4)

    def y_peer(i):
        return lax.rem(y + i, 4) * 4 + x

    near = (x_peer, y_peer)

    bar = pltpu.get_barrier_semaphore()
    partners = [nxt_id, prv_id, (lax.rem(z + 1, 4) * 2 + core, c), (lax.rem(z + 3, 4) * 2 + core, c)]
    partners += [(r, peer(i)) for i in (2, 1, 3) for peer in near] + [sibling]
    for dev in partners:
        pl.semaphore_signal(bar, inc=1, device_id=dev, device_id_type=MESH)

    fetch = {}
    vm = dict(
        atoms=ext.at[pl.ds(REACH, A)], abias=abias, kmask=kmask, atok=tk, tokens=tokens, pbias=pbias, tmask=tmask,
        aq=aq, akv=akv, ag=ag, ao=ao, pool=pool, tq=tq, tkv=tkv, tg=tg, to=to, rg=rg, ru=ru, rd=rd,
    )
    for i, name in enumerate(EARLY + LATE):
        fetch[name] = pltpu.make_async_copy(hbm[name], vm[name], in_sem.at[i])
    for name in EARLY:
        fetch[name].start()

    for name in ("atoms", "akv", "aq", "ag"):
        fetch[name].wait()
    own_f = ext[pl.ds(REACH, A), :].astype(F32)
    own_n = norm(own_f).astype(BF16)
    q_a = dot(own_n, aq[...]).astype(BF16)
    gate_a = sigmoid(dot(own_n, ag[...]))
    kv_own = dot(own_n, akv[...]).astype(BF16)
    fetch["kmask"].wait()
    fetch["abias"].wait()
    p_r = iota((HA * WQ, HA * WQ), 0)
    p_c = iota((HA * WQ, HA * WQ), 1)
    perm = (p_c == lax.rem(p_r, WQ) * HA + p_r // WQ).astype(F32).astype(BF16)
    bias_w = [dot(perm, abias[pl.ds(HA * WQ * w, HA * WQ), :]) for w in range(A // WQ)]
    lane = iota((1, WK), 1)
    head_f = [jnp.where((lane // DA) == h, 1.0, 0.0).astype(F32) for h in range(HA)]
    head_b = [f.astype(BF16) for f in head_f]

    def window(w, kv):
        q_w = q_a[WQ * w : WQ * (w + 1)]
        q_bd = jnp.concatenate([q_w * head_b[h] for h in range(HA)], axis=0)
        s = lax.dot_general(q_bd, kv[:, :WK], (((1,), (1,)), ((), ())), preferred_element_type=F32)
        s = s * (DA**-0.5) + bias_w[w]
        pos = lin * A + WQ * w + lane - REACH
        valid = (kmask[pl.ds(w, 1), :] == 1) & (pos >= 0) & (pos < TOTAL_ATOMS)
        s = jnp.where(valid, s, MASKED)
        e = jnp.exp(s - jnp.max(s, axis=-1, keepdims=True))
        t = jnp.sum(e, axis=-1, keepdims=True)
        o = dot(e.astype(BF16), kv[:, WK:]) / t
        return sum(o[WQ * h : WQ * (h + 1)] * head_f[h] for h in range(HA))

    def mid_of(first, attended):
        rows = slice(first, first + WQ * len(attended))
        gated = (jnp.concatenate(attended, axis=0) * gate_a[rows]).astype(BF16)
        return (own_f[rows] + dot(gated, ao[...])).astype(BF16)

    fetch["ao"].wait()
    g_mid[c, 0:H, :] = mid_of(64, [window(w, kv_own[WQ * w - REACH : WQ * w - REACH + WK]) for w in (2, 3, 4, 5)])
    fetch["atok"].wait()
    turned = pltpu.roll(jnp.broadcast_to(tk[...] - r * T, (8, A)), 64, 1)
    line = iota((16, 128), 0)
    number = jnp.where(lax.rem(line, 2) == 0, turned[0:1, H:], turned[0:1, :H])
    number = jnp.where(line < 2, number >> 1, number & 1)
    g_mid[c, H:HEAD, :] = jnp.where(line < 4, number, 0).astype(F32).astype(BF16)
    pl.semaphore_wait(bar, len(partners))

    halo = [
        remote(ext.at[pl.ds(A, REACH)], ext.at[pl.ds(0, REACH)], halo_s.at[0], halo_r.at[0], nxt_id),
        remote(ext.at[pl.ds(REACH, REACH)], ext.at[pl.ds(REACH + A, REACH)], halo_s.at[1], halo_r.at[1], prv_id),
    ]
    for cp in halo:
        cp.start()

    def mid_at(half, s):
        return g_mid.at[s, pl.ds(HEAD * half, HEAD - 16 * half)]

    def mid_copy(half, s, slot, dev):
        return remote(mid_at(half, s), mid_at(half, s), mid_s.at[half, slot], mid_r.at[half, s], (r, dev))

    def own_hops(half, send):
        for i in (2, 1, 3):
            send(half, c, i - 1, near[half](i))
        for i in (2, 1, 3):
            send(half, c, i + 2, near[1 - half](i))

    def next_hops(half, k, wait, send):
        s = near[half]((1, 3, 2)[k])
        if wait is not None:
            wait(half, s, 0, c).wait_recv()
        for i in (2, 1, 3):
            send(half, s, 3 * k + i + 5, near[1 - half](i))

    def all_hops(half, send):
        own_hops(half, send)
        for k in range(3):
            next_hops(half, k, None, send)

    def mid_start(half, s, slot, dev):
        mid_copy(half, s, slot, dev).start()

    def onward(half):
        for k in range(3):
            next_hops(half, k, mid_copy, mid_start)

    own_hops(0, mid_start)
    for name in LATE:
        fetch[name].start()
    onward(0)
    edges = []
    for side in range(2):
        halo[side].wait_recv()
        edge = norm(ext[pl.ds((REACH + A) * side, REACH), :].astype(F32)).astype(BF16)
        inside = jnp.where(lin == (ROWS * COLS - 1) * side, 0.0, 1.0).astype(F32)
        edges.append((dot(edge, akv[...]) * inside).astype(BF16))
    near_by = jnp.concatenate([kv_own[6 * WQ - REACH :], edges[1]], axis=0)
    g_mid[c, HEAD : HEAD + 64, :] = mid_of(192, [window(6, near_by[:WK]), window(7, near_by[WQ : WQ + WK])])
    near_by = jnp.concatenate([edges[0], kv_own[: WK - WQ + 16]], axis=0)
    g_mid[c, HEAD + 64 :, :] = mid_of(0, [window(0, near_by[:WK]), window(1, near_by[WQ : WQ + WK])])
    own_hops(1, mid_start)
    mid_out_copies = [
        pltpu.make_async_copy(g_mid.at[c, pl.ds(a, n)], mid_out.at[pl.ds(b, n)], own_sem.at[i])
        for i, (a, b, n) in enumerate(((0, 64, H), (HEAD, 192, 64), (HEAD + 64, 0, 64)))
    ]
    for cp in mid_out_copies:
        cp.start()

    fetch["pool"].wait()

    key_off = lax.rem(c, 2) * K

    def step_blocks(half, step):
        o = lax.rem(step * (step + 1) // 2, 4)
        if half == 0:
            return [lax.rem(y + o, 4) * 4 + b for b in range(4)]
        return [b * 4 + lax.rem(x + o, 4) for b in range(4)]

    def selector(half, step, off):
        at = (iota((K, H), 0) + off).astype(F32)
        sel = []
        for s in step_blocks(half, step):
            terms = g_mid[s, H:HEAD, :].astype(F32)
            number = 2.0 * terms[half : half + 1] + terms[2 + half : 3 + half]
            sel.append(jnp.where(at == number, 1.0, 0.0).astype(F32))
        return sel

    def feat_rows(half, step, n):
        return pl.ds(pl.multiple_of((4 * half + step) * 512, 512), 512 * n)

    def pool_into(off, sel, f):
        rows = pl.ds(pl.multiple_of(off, K), K)
        count = sel[0]
        for m in sel[1:]:
            count = count + m
        selsum[rows, :] += count
        acc[rows, :] += dot(jnp.concatenate([m.astype(BF16) for m in sel], axis=1), f)

    def pool_step(half, wait, step, carry):
        blocks = step_blocks(half, step)
        if wait:
            for s in blocks:
                mid_copy(half, s, 0, s).wait_recv()
        f = jnp.concatenate([g_mid[s, pl.ds(HEAD * half, H), :] for s in blocks], axis=0)
        f = jnp.maximum(dot(f, pool[...]), 0.0).astype(BF16)
        feats[feat_rows(half, step, 1), :] = f
        pool_into(key_off, selector(half, step, key_off), f)
        return carry

    acc[...] = jnp.zeros(acc.shape, F32)
    selsum[...] = jnp.zeros(selsum.shape, F32)
    for half in range(2):
        pool_step(half, False, 0, 0)
        if half == 0:
            onward(1)
        lax.fori_loop(1, 4, functools.partial(pool_step, half, True), 0)
    fetch["tokens"].wait()
    ones = jnp.ones((H, 128), BF16)

    def finish_chunk(first):
        rows = pl.ds(pl.multiple_of(first, 128), 128)
        inv = 1.0 / dot(selsum[rows, :].astype(BF16), ones)
        inv = jnp.concatenate([inv] * (C // 128), axis=1)
        m = (tokens[rows, :].astype(F32) + acc[rows, :] * inv).astype(BF16)
        tmid[rows, :] = m
        tnorm[rows, :] = norm(m.astype(F32)).astype(BF16)

    z0, core0 = (c // 2) // 2, lax.rem(c // 2, 2)
    away = lax.rem(z - z0 + 4, 4)
    on_core = core == core0
    is_src = on_core & (away == 0)
    is_sib = jnp.logical_not(on_core) & (away == 0)
    odd = jnp.where(on_core, 0, 1)
    swap = jnp.where(away == 3, 1, 0)
    up, down = (lax.rem(z + 1, 4) * 2 + core, c), (lax.rem(z + 3, 4) * 2 + core, c)
    onward_id = (lax.rem(z + away, 4) * 2 + core, c)

    def key_copy(q, slot, dev):
        rows = knorm.at[pl.ds(pl.multiple_of(q * OWN, OWN), OWN)]
        return remote(rows, rows, key_s.at[q, slot], key_r.at[q], dev)

    def chip_part(n):
        return 2 * lax.rem(n + 2 * swap, 4) + odd

    for pair in range(2):
        finish_chunk(key_off + 128 * pair)

        @pl.when(is_src)
        def _():
            rows = pl.ds(pl.multiple_of(key_off + 128 * pair, 128), 128)
            knorm[pl.ds(128 * pair, 128), :] = tnorm[rows, :]
            q = 4 * pair
            for p in (q + 1, q + 3):
                key_copy(p, 2, sibling).start()
            for p in (q, q + 2):
                key_copy(p, 0, up).start()
            if pair == 1:
                for p in (4, 6, 0, 2):
                    key_copy(p, 1, down).start()
            for p in (q, q + 2):
                key_copy(p, 2, sibling).start()

    @pl.when(is_sib)
    def _():
        for p in (1, 3, 5, 7):
            key_copy(p, 0, up).wait_recv()
            key_copy(p, 0, up).start()
            if p > 4:
                key_copy(p, 1, down).start()
        for p in (1, 3):
            key_copy(p, 1, down).start()

    other_off = K - key_off

    def other_step(half, step, carry):
        sel = selector(half, 2 * step, other_off) + selector(half, 2 * step + 1, other_off)
        pool_into(other_off, sel, feats[feat_rows(half, 2 * step, 2), :])
        return carry

    for half in range(2):
        lax.fori_loop(0, 2, functools.partial(other_step, half), 0)
    own_rows = pl.ds(pl.multiple_of(c * OWN, OWN), OWN)
    for n in range(4):

        @pl.when(away != 0)
        def _():
            key_copy(chip_part(n), 2, sibling).wait_recv()
            key_copy(chip_part(n), 2, sibling).start()

        if n < 2:

            @pl.when((away == 1) | (away == 3))
            def _():
                key_copy(chip_part(n), 0, onward_id).start()

        if n < 2:
            finish_chunk(other_off + 128 * n)
        else:
            if n == 2:
                fetch["tq"].wait()
            for i in (2 * n - 4, 2 * n - 3):
                q_s[pl.ds(128 * i, 128), :] = dot(tnorm[pl.ds(128 * i, 128), :], tq[...]).astype(BF16)

    @pl.when(jnp.logical_not(is_src))
    def _():
        for n in range(4):
            q = 2 * n + 1 - odd
            key_copy(q, 2, sibling).wait_recv()

    fetch["tkv"].wait()
    kt = (dot(knorm[...], tkv[:, :C]) * (DT**-0.5)).T
    row_i = iota((C, 1), 0)
    v_full = dot(knorm[...], tkv[:, C:])
    lane_i = iota((1, C), 1)
    for g in range(2):
        for h in range(8):
            b0, n = SPANS[h]
            lo, hi = G * g + 128 * b0, G * g + 128 * (b0 + n)
            start = G * g + DT * h
            rm = (row_i[lo:hi] >= start) & (row_i[lo:hi] < start + DT)
            kt_s[8 * g + h, pl.ds(0, 128 * n), :] = jnp.where(rm, kt[lo:hi], 0.0).astype(BF16)
            lm = (lane_i[:, lo:hi] >= start) & (lane_i[:, lo:hi] < start + DT)
            v_s[8 * g + h, :, pl.ds(0, 128 * n)] = jnp.where(lm, v_full[:, lo:hi], 0.0).astype(BF16)
    fetch["tmask"].wait()
    fetch["pbias"].wait()

    def one_copy(g, d):
        return remote(snd.at[g, d], rcv.at[g, lax.rem(c // (1 + 3 * g), 4)], one_s.at[g, d],
                      one_r.at[g, lax.rem(c // (1 + 3 * g), 4)], (r, (y * 4 + d) * (1 - g) + (d * 4 + x) * g))

    def attend(offsets, g, carry):
        me = lax.rem(c // (1 + 3 * g), 4)
        dests = [lax.rem(me + o, 4) for o in offsets]
        size = 128 * len(dests)
        rows = [
            pl.ds(pl.multiple_of((b * (4 - 3 * g) + d * (1 + 3 * g)) * OWN, OWN), OWN) for d in dests for b in range(4)
        ]
        live = tmask[...] == 1
        lane8 = lax.rem(iota((size, 128), 1), 8)
        parts = [None] * 3
        stat = jnp.zeros((size, 128), F32)
        for h in range(8):
            b0, n = SPANS[h]
            lanes = pl.ds(pl.multiple_of(g * G + 128 * b0, 128), 128 * n)
            qw = jnp.concatenate([q_s[rw, lanes] for rw in rows], axis=0)
            s = dot(qw, kt_s[g * 8 + h, pl.ds(0, 128 * n), :])
            s = s + jnp.concatenate([pbias[g * 8 + h, rw, :] for rw in rows], axis=0).astype(F32)
            s = jnp.where(live, s, MASKED)
            top = jnp.max(s, axis=-1, keepdims=True)
            e = jnp.exp(s - top)
            total = jnp.sum(e, axis=-1, keepdims=True)
            o = dot(e.astype(BF16), v_s[g * 8 + h, :, pl.ds(0, 128 * n)]) * (1.0 / total)
            for b in range(n):
                ob = o[:, 128 * b : 128 * (b + 1)]
                parts[b0 + b] = ob if parts[b0 + b] is None else parts[b0 + b] + ob
            stat = jnp.where(lane8 == h, top + jnp.log(total), stat)
        stat = split_lse(stat)
        for n, d in enumerate(dests):
            for b in range(3):
                snd[g, d, pl.ds(128 * b, 128), :] = parts[b][128 * n : 128 * (n + 1)].astype(BF16)
            snd[g, d, pl.ds(G, 32), :] = stat[128 * n : 128 * (n + 1)].T[:32].astype(BF16)

            if offsets[n] != 0:
                one_copy(g, d).start()

        return carry

    for offsets in ((2,), (1, 3), (0,)):
        lax.fori_loop(0, 2, functools.partial(attend, offsets), 0)

    fetch["tg"].wait()
    gate_t = sigmoid(dot(tnorm[own_rows, :], tg[...]))
    mine = (x, y)
    join = join_lse()

    def two_copy(g, d):
        dev = (r, d * 4 + x) if g == 0 else (r, y * 4 + d)
        me = mine[1 - g]
        return remote(snd2.at[g, d], rcv2.at[g, me], two_s.at[g, d], two_r.at[g, me], dev)

    for g in range(2):
        blocks = [snd[g, mine[g]]]
        for i in (2, 3, 1):
            d = lax.rem(mine[g] + i, 4)
            remote(snd.at[g, d], rcv.at[g, d], one_s.at[g, d], one_r.at[g, d], (r, near[g](i))).wait_recv()
            blocks.append(rcv[g, d])
        values = [jnp.concatenate([b[128 * k : 128 * (k + 1)] for k in range(3)], axis=1) for b in blocks]
        lse = [
            lax.dot_general(b[G:], join[:32], (((0,), (0,)), ((), ())), preferred_element_type=F32) for b in blocks
        ]
        half_merged = merge(values, lse, True)
        for d in range(4):
            snd2[g, d] = half_merged[OWN * d : OWN * (d + 1)]
        for i in (2, 1, 3):
            two_copy(g, lax.rem(mine[1 - g] + i, 4)).start()
    merged = []
    for g in range(2):
        blocks = [snd2[g, mine[1 - g]]]
        for i in (1, 3, 2):
            d = lax.rem(mine[1 - g] + i, 4)
            remote(snd2.at[g, d], rcv2.at[g, d], two_s.at[g, d], two_r.at[g, d], (r, near[1 - g](i))).wait_recv()
            blocks.append(rcv2[g, d])
        merged.append(merge([b[:, :G] for b in blocks], [dot(b[:, G:], join) for b in blocks], False))
    att = jnp.concatenate(merged, axis=1)

    for name in ("to", "rg", "ru", "rd"):
        fetch[name].wait()
    gated = (att * gate_t).astype(BF16)
    t_att = (tmid[own_rows, :].astype(F32) + dot(gated, to[...])).astype(BF16)
    n_att = norm(t_att.astype(F32)).astype(BF16)
    up = dot(n_att, rg[...])
    hid = (up * sigmoid(up) * dot(n_att, ru[...])).astype(BF16)
    t_new = (t_att.astype(F32) + dot(hid, rd[...])).astype(BF16)
    g_new[own_rows, :] = t_new

    def rows_of(half, s):
        return pl.ds(pl.multiple_of(s * OWN + 16 * half, 16), 16)

    def new_copy(half, s, slot, dev):
        dst = g_new if slot < 3 else tokens_out
        return remote(
            g_new.at[rows_of(half, s)], dst.at[rows_of(half, s)], new_s.at[half, slot], new_r.at[half, s], (r, dev)
        )

    out_copies = [pltpu.make_async_copy(g_new.at[own_rows], tokens_out.at[own_rows], own_sem.at[3])]
    def new_start(half, s, slot, dev):
        new_copy(half, s, slot, dev).start()

    for half in range(2):
        own_hops(half, new_start)
    out_copies[0].start()
    for half in range(2):
        for k, i in enumerate((1, 3, 2)):
            rows = rows_of(half, near[half](i))
            out_copies.append(pltpu.make_async_copy(g_new.at[rows], tokens_out.at[rows], own_sem.at[4 + 3 * half + k]))

    for k in range(3):
        for half in range(2):
            next_hops(half, k, new_copy, new_start)
    for cp in out_copies[1:]:
        cp.start()

    for half in range(2):
        for i in (1, 3, 2):
            for j in range(4):
                s = y_peer(i) // 4 * 4 + j if half == 0 else j * 4 + lax.rem(x + i, 4)
                new_copy(half, s, 3, s).wait_recv()
    for cp in mid_out_copies + out_copies:
        cp.wait()
    for cp in halo:
        cp.wait_send()

    def sent(half, s, slot, dev):
        mid_copy(half, s, slot, dev).wait_send()
        new_copy(half, s, slot, dev).wait_send()

    for half in range(2):
        all_hops(half, sent)
    for g in range(2):
        for i in (1, 3, 2):
            one_copy(g, lax.rem(mine[g] + i, 4)).wait_send()
            two_copy(g, lax.rem(mine[1 - g] + i, 4)).wait_send()

    @pl.when(is_src)
    def _():
        for q in range(8):
            key_copy(q, 2, sibling).wait_send()
            if q % 2 == 0:
                key_copy(q, 0, up).wait_send()
                key_copy(q, 1, down).wait_send()

    @pl.when(is_sib)
    def _():
        for q in (1, 3, 5, 7):
            key_copy(q, 0, up).wait_send()
            key_copy(q, 1, down).wait_send()

    @pl.when(away != 0)
    def _():
        for n in range(4):
            key_copy(chip_part(n), 2, sibling).wait_send()

    @pl.when((away == 1) | (away == 3))
    def _():
        for n in (0, 1):
            key_copy(chip_part(n), 0, onward_id).wait_send()


def to_atoms(mid, new, back, atok, atoms_out, tokens_out, mid_v, new_v, back_v, atok_v, in_sem, out_sem):
    n = 8
    rows = [pl.ds(i * (T // n), T // n) for i in range(n)]
    ins = [pltpu.make_async_copy(new.at[w], new_v.at[w], in_sem.at[i]) for i, w in enumerate(rows)]
    small = [
        pltpu.make_async_copy(a, b, in_sem.at[n + i])
        for i, (a, b) in enumerate(((atok, atok_v), (back, back_v), (mid, mid_v)))
    ]
    outs = [pltpu.make_async_copy(new_v.at[w], tokens_out.at[w], out_sem.at[i]) for i, w in enumerate(rows)]
    for cp in ins[:2] + small + ins[2:]:
        cp.start()
    first = lax.axis_index("row") * T
    lane = iota((A, 128), 1).astype(F32)
    ins[0].wait()
    outs[0].start()
    for cp in small:
        cp.wait()
    tok_t = jnp.broadcast_to((atok_v[...] - first).astype(F32), (128, A)).T
    update = None
    for i, w in enumerate(rows):
        if i > 0:
            ins[i].wait()
            outs[i].start()
        if i % 2 == 1:
            w = pl.ds(T // n * (i - 1), 128)
            pick = jnp.where(tok_t == lane + float(T // n * (i - 1)), 1.0, 0.0).astype(BF16)
            term = dot(pick, dot(new_v[w, :], back_v[...]).astype(BF16))
            update = term if update is None else update + term
    mid_v[...] = (mid_v[...].astype(F32) + update).astype(BF16)
    last = pltpu.make_async_copy(mid_v, atoms_out, out_sem.at[n])
    last.start()
    for cp in outs + [last]:
        cp.wait()


def on_device(
    atoms, atom_bias, key_mask, atom_token, tokens, pair_bias, token_mask,
    atom_query, atom_keyval, atom_gate, atom_out, pool_weight,
    token_query, token_keyval, token_gate, token_out, trans_gate, trans_up, trans_down, back_weight,
):
    atok = atom_token.reshape(1, A)
    args = (
        atoms, atom_bias.reshape(A * HA, WK), key_mask, atok, tokens, pair_bias,
        token_mask.reshape(1, K), atom_query, atom_keyval, atom_gate, atom_out, pool_weight,
        token_query, token_keyval, token_gate, token_out, trans_gate, trans_up, trans_down,
    )
    vmem = [pltpu.VMEM(a.shape, a.dtype) for a in args]
    vmem[0] = pltpu.VMEM((A + 2 * REACH, 128), BF16)
    dma = pltpu.SemaphoreType.DMA
    scratch = vmem + [
        pltpu.VMEM((COLS, A + 16, 128), BF16),
        pltpu.VMEM((COLS * A, C), BF16),
        pltpu.VMEM((T, C), F32),
        pltpu.VMEM((T, H), F32),
        pltpu.VMEM((T, C), BF16),
        pltpu.VMEM((T, C), BF16),
        pltpu.VMEM((K, C), BF16),
        pltpu.VMEM((T, C), BF16),
        pltpu.VMEM((16, 256, K), BF16),
        pltpu.VMEM((16, K, 256), BF16),
        pltpu.VMEM((2, 4, G + 32, 128), BF16),
        pltpu.VMEM((2, 4, G + 32, 128), BF16),
        pltpu.VMEM((2, 4, OWN, G + 128), BF16),
        pltpu.VMEM((2, 4, OWN, G + 128), BF16),
        pltpu.VMEM((T, C), BF16),
        dma((len(args),)), dma((2,)), dma((2,)),
        dma((2, COLS)), dma((2, COLS)),
        dma((8, 3)), dma((8,)),
        dma((2, 4)), dma((2, 4)), dma((2, 4)), dma((2, 4)),
        dma((2, COLS)), dma((2, COLS)), dma((10,)),
    ]
    mid, new = pl.pallas_call(
        kernel,
        out_shape=(jax.ShapeDtypeStruct((A, 128), BF16), jax.ShapeDtypeStruct((T, C), BF16)),
        in_specs=[pl.BlockSpec(memory_space=pl.ANY)] * len(args),
        out_specs=(pl.BlockSpec(memory_space=pl.ANY),) * 2,
        scratch_shapes=scratch,
        compiler_params=pltpu.CompilerParams(
            collective_id=0, has_side_effects=True, vmem_limit_bytes=60 * 1024 * 1024
        ),
        name="block",
    )(*args)
    hbm = pl.BlockSpec(memory_space=pl.ANY)
    return pl.pallas_call(
        to_atoms,
        out_shape=(jax.ShapeDtypeStruct((A, 128), BF16), jax.ShapeDtypeStruct((T, C), BF16)),
        in_specs=[hbm] * 4,
        out_specs=(hbm, hbm),
        scratch_shapes=[
            pltpu.VMEM((A, 128), BF16), pltpu.VMEM((T, C), BF16), pltpu.VMEM((C, 128), BF16), pltpu.VMEM((1, A), jnp.int32),
            dma((11,)), dma((9,)),
        ],
        compiler_params=pltpu.CompilerParams(vmem_limit_bytes=60 * 1024 * 1024),
        name="to_atoms",
    )(mid, new, back_weight, atok)


def solution(mesh):
    both = ("row", "col")
    in_specs = (
        P(both, None), P(both, None, None), P(both, None), P(both), P("row", None), P(None, "row", "col"), P("col"),
    ) + (P(),) * 13
    out_specs = (P(both, None), P("row", None))
    return jax.shard_map(on_device, mesh=mesh, in_specs=in_specs, out_specs=out_specs, check_vma=False)
```

```python
import functools

import jax
import jax.numpy as jnp
from jax import lax
from jax.experimental import pallas as pl
from jax.experimental.pallas import tpu as pltpu
from jax.sharding import PartitionSpec as P

F32 = jnp.float32
BF16 = jnp.bfloat16
MESH = pl.DeviceIdType.MESH
ROWS, COLS = 8, 16
EPSILON = 1e-05
MASKED = -1000000000.0
HA, DA, WQ, WK = 4, 32, 32, 128
DT = 48
REACH = 48
A = 256
T = 512
PIECES = ((0, 80), (80, 80), (160, 64), (224, 64))
K = 256
C = 768
G = 384
OWN = 32
H = 128
TOTAL_ATOMS = 32768


def dot(a, b):
    return jnp.dot(a, b, preferred_element_type=F32)


def norm(x):
    mean = jnp.mean(x, axis=-1, keepdims=True)
    d = x - mean
    var = jnp.mean(d * d, axis=-1, keepdims=True)
    return d * lax.rsqrt(var + EPSILON)


def sigmoid(x):
    return 1.0 / (1.0 + jnp.exp(-x))


def iota(shape, dim):
    return lax.broadcasted_iota(jnp.int32, shape, dim)


IN_NAMES = (
    "atoms", "abias", "kmask", "atok", "tokens", "pbias", "tmask", "aq", "akv", "ag", "ao", "pool",
    "tq", "tkv", "tg", "to", "rg", "ru", "rd",
)
EARLY = ("atoms", "akv", "aq", "ag", "kmask", "abias", "ao", "atok", "pool")
LATE = ("tokens", "tg", "tq", "tkv", "tmask", "pbias", "to", "rg", "ru", "rd")
SPANS = tuple(((DT * h) // 128, (DT * h + DT - 1) // 128 - (DT * h) // 128 + 1) for h in range(8))


def split_lse(stat):
    high = stat.astype(BF16).astype(F32)
    rest = stat - high
    middle = rest.astype(BF16).astype(F32)
    third = iota(stat.shape, 1) // 8
    return jnp.where(third == 0, high, jnp.where(third == 1, middle, rest - middle))


def join_lse():
    l_r, l_c = iota((128, 128), 0), iota((128, 128), 1)
    return jnp.where((l_r < 24) & (lax.rem(l_r, 8) == lax.rem(l_c, 8)), 1.0, 0.0).astype(BF16)


def merge(values, lse, want_lse):
    s_r, s_c = iota((128, G), 0), iota((128, G), 1)
    spread = jnp.where((s_r < 16) & (lax.rem(s_r, 8) == s_c // DT), 1.0, 0.0).astype(BF16)
    top = lse[0]
    for l in lse[1:]:
        top = jnp.maximum(top, l)
    wgt = [jnp.exp(l - top) for l in lse]
    total = wgt[0]
    for w in wgt[1:]:
        total = total + w
    inv = 1.0 / total
    first = iota(top.shape, 1) < 8
    out = None
    for w, v in zip(wgt, values):
        w = w * inv
        high = w.astype(BF16).astype(F32)
        term = dot(jnp.where(first, high, w - high).astype(BF16), spread) * v.astype(F32)
        out = term if out is None else out + term
    if want_lse:
        return jnp.concatenate([out, split_lse(top + jnp.log(total))], axis=1).astype(BF16)
    return out


def kernel(*refs):
    n_in = len(IN_NAMES)
    hbm = dict(zip(IN_NAMES, refs[:n_in]))
    mid_out, tokens_out = refs[n_in : n_in + 2]
    (
        ext, abias, kmask, tk, tokens, pbias, tmask, aq, akv, ag, ao, pool, tq, tkv, tg, to, rg, ru, rd,
        g_mid, feats, acc, selsum, tmid, tnorm, knorm, q_s, kt_s, v_s, snd, rcv, snd2, rcv2, g_new,
        in_sem, halo_s, halo_r, mid_s, mid_r, key_s, key_r,
        one_s, one_r, two_s, two_r, new_s, new_r, own_sem,
    ) = refs[n_in + 2 :]

    r = lax.axis_index("row")
    c = lax.axis_index("col")
    y, x = c // 4, lax.rem(c, 4)
    z, core = r // 2, lax.rem(r, 2)
    lin = r * COLS + c
    nxt = lax.rem(lin + 1, ROWS * COLS)
    prv = lax.rem(lin + ROWS * COLS - 1, ROWS * COLS)
    nxt_id = (nxt // COLS, lax.rem(nxt, COLS))
    prv_id = (prv // COLS, lax.rem(prv, COLS))
    sibling = (z * 2 + 1 - core, c)

    def remote(src, dst, ss, rs, dev):
        return pltpu.make_async_remote_copy(
            src_ref=src, dst_ref=dst, send_sem=ss, recv_sem=rs, device_id=dev, device_id_type=MESH
        )

    def x_peer(i):
        return y * 4 + lax.rem(x + i, 4)

    def y_peer(i):
        return lax.rem(y + i, 4) * 4 + x

    near = (x_peer, y_peer)

    bar = pltpu.get_barrier_semaphore()
    partners = [nxt_id, prv_id, (lax.rem(z + 1, 4) * 2 + core, c), (lax.rem(z + 3, 4) * 2 + core, c)]
    partners += [(r, peer(i)) for i in (2, 1, 3) for peer in near] + [sibling]
    for dev in partners:
        pl.semaphore_signal(bar, inc=1, device_id=dev, device_id_type=MESH)

    fetch = {}
    vm = dict(
        atoms=ext.at[pl.ds(REACH, A)], abias=abias, kmask=kmask, atok=tk, tokens=tokens, pbias=pbias, tmask=tmask,
        aq=aq, akv=akv, ag=ag, ao=ao, pool=pool, tq=tq, tkv=tkv, tg=tg, to=to, rg=rg, ru=ru, rd=rd,
    )
    for i, name in enumerate(EARLY + LATE):
        fetch[name] = pltpu.make_async_copy(hbm[name], vm[name], in_sem.at[i])
    for name in EARLY:
        fetch[name].start()

    for name in ("atoms", "akv", "aq", "ag"):
        fetch[name].wait()
    own_f = ext[pl.ds(REACH, A), :].astype(F32)
    own_n = norm(own_f).astype(BF16)
    q_a = dot(own_n, aq[...]).astype(BF16)
    gate_a = sigmoid(dot(own_n, ag[...]))
    kv_own = dot(own_n, akv[...]).astype(BF16)
    fetch["kmask"].wait()
    fetch["abias"].wait()
    p_r = iota((HA * WQ, HA * WQ), 0)
    p_c = iota((HA * WQ, HA * WQ), 1)
    perm = (p_c == lax.rem(p_r, WQ) * HA + p_r // WQ).astype(F32).astype(BF16)
    bias_w = [dot(perm, abias[pl.ds(HA * WQ * w, HA * WQ), :]) for w in range(A // WQ)]
    lane = iota((1, WK), 1)
    head_f = [jnp.where((lane // DA) == h, 1.0, 0.0).astype(F32) for h in range(HA)]
    head_b = [f.astype(BF16) for f in head_f]

    def window(w, kv):
        q_w = q_a[WQ * w : WQ * (w + 1)]
        q_bd = jnp.concatenate([q_w * head_b[h] for h in range(HA)], axis=0)
        s = lax.dot_general(q_bd, kv[:, :WK], (((1,), (1,)), ((), ())), preferred_element_type=F32)
        s = s * (DA**-0.5) + bias_w[w]
        pos = lin * A + WQ * w + lane - REACH
        valid = (kmask[pl.ds(w, 1), :] == 1) & (pos >= 0) & (pos < TOTAL_ATOMS)
        s = jnp.where(valid, s, MASKED)
        e = jnp.exp(s - jnp.max(s, axis=-1, keepdims=True))
        t = jnp.sum(e, axis=-1, keepdims=True)
        o = dot(e.astype(BF16), kv[:, WK:]) / t
        return sum(o[WQ * h : WQ * (h + 1)] * head_f[h] for h in range(HA))

    def mid_of(first, attended):
        rows = slice(first, first + WQ * len(attended))
        gated = (jnp.concatenate(attended, axis=0) * gate_a[rows]).astype(BF16)
        return (own_f[rows] + dot(gated, ao[...])).astype(BF16)

    def put(piece, rows):
        g_mid[c, PIECES[piece][0] : PIECES[piece][0] + 64, :] = rows

    fetch["ao"].wait()
    inner = mid_of(64, [window(w, kv_own[WQ * w - REACH : WQ * w - REACH + WK]) for w in (2, 3, 4, 5)])
    put(0, inner[:64])
    put(1, inner[64:])
    fetch["atok"].wait()
    numbers = jnp.broadcast_to(tk[...] - r * T, (16, A))
    turned, rest = pltpu.roll(numbers[:, :H], 64, 1), numbers[:, H:]
    left = iota((16, H), 1) < 64
    line = iota((16, H), 0)
    for piece in range(2):
        number = jnp.where(left, turned, rest) if piece == 0 else jnp.where(left, rest, turned)
        number = jnp.where(line == 0, number >> 1, jnp.where(line == 1, number & 1, 0))
        g_mid[c, 64 + 80 * piece : 80 + 80 * piece, :] = number.astype(F32).astype(BF16)
    pl.semaphore_wait(bar, len(partners))

    halo = [
        remote(ext.at[pl.ds(A, REACH)], ext.at[pl.ds(0, REACH)], halo_s.at[0], halo_r.at[0], nxt_id),
        remote(ext.at[pl.ds(REACH, REACH)], ext.at[pl.ds(REACH + A, REACH)], halo_s.at[1], halo_r.at[1], prv_id),
    ]
    for cp in halo:
        cp.start()

    def mid_copy(piece, s, slot, dev):
        rows = g_mid.at[s, pl.ds(*PIECES[piece])]
        return remote(rows, rows, mid_s.at[piece, slot], mid_r.at[piece, s], (r, dev))

    def own_hops(piece, send):
        half = piece % 2
        for i in (2, 1, 3):
            send(piece, c, i - 1, near[half](i))
        for i in (2, 1, 3):
            send(piece, c, i + 2, near[1 - half](i))

    def next_hops(piece, k, wait, send):
        half = piece % 2
        s = near[half]((1, 3, 2)[k])
        if wait is not None:
            wait(piece, s, 0, c).wait_recv()
        for i in (2, 1, 3):
            send(piece, s, 3 * k + i + 5, near[1 - half](i))

    def all_hops(piece, send):
        own_hops(piece, send)
        for k in range(3):
            next_hops(piece, k, None, send)

    def mid_start(piece, s, slot, dev):
        mid_copy(piece, s, slot, dev).start()

    def onward(pieces):
        for k in range(3):
            for piece in pieces:
                next_hops(piece, k, mid_copy, mid_start)

    own_hops(0, mid_start)
    own_hops(1, mid_start)
    for name in LATE:
        fetch[name].start()
    onward((0, 1))
    edges = []
    for side in range(2):
        halo[side].wait_recv()
        edge = norm(ext[pl.ds((REACH + A) * side, REACH), :].astype(F32)).astype(BF16)
        inside = jnp.where(lin == (ROWS * COLS - 1) * side, 0.0, 1.0).astype(F32)
        edges.append((dot(edge, akv[...]) * inside).astype(BF16))
    near_by = jnp.concatenate([kv_own[6 * WQ - REACH :], edges[1]], axis=0)
    put(2, mid_of(192, [window(6, near_by[:WK]), window(7, near_by[WQ : WQ + WK])]))
    own_hops(2, mid_start)
    near_by = jnp.concatenate([edges[0], kv_own[: WK - WQ + 16]], axis=0)
    put(3, mid_of(0, [window(0, near_by[:WK]), window(1, near_by[WQ : WQ + WK])]))
    own_hops(3, mid_start)
    mid_out_copies = [
        pltpu.make_async_copy(g_mid.at[c, pl.ds(PIECES[i][0], 64)], mid_out.at[pl.ds(b, 64)], own_sem.at[i])
        for i, b in enumerate((64, 128, 192, 0))
    ]
    for cp in mid_out_copies:
        cp.start()

    fetch["pool"].wait()

    key_off = lax.rem(c, 2) * K

    def step_blocks(step):
        o = lax.rem(step * (step + 1) // 2, 4)
        return [lax.rem(y + o, 4) * 4 + b for b in range(4)], [b * 4 + lax.rem(x + o, 4) for b in range(4)]

    def selector(late, step, off):
        at = (iota((K, H), 0) + off).astype(F32)
        left = iota((8, H), 1) < 64
        sel = []
        for half, blocks in enumerate(step_blocks(step)):
            numbers = []
            for s in blocks:
                terms = g_mid[s, 64 + 80 * half : 80 + 80 * half, :].astype(F32)
                numbers.append(jnp.broadcast_to(2.0 * terms[0:1] + terms[1:2], (8, H)))
            for n in (0, 2):
                if late:
                    pair = jnp.where(left, pltpu.roll(numbers[n], 64, 1), numbers[n + 1])
                else:
                    pair = jnp.where(left, numbers[n], pltpu.roll(numbers[n + 1], 64, 1))
                sel.append(jnp.where(at == pair[0:1], 1.0, 0.0).astype(F32))
        return sel

    def feat_rows(half, step, n):
        return pl.ds(pl.multiple_of((4 * half + step) * 512, 512), 512 * n)

    def pool_into(off, sel, f):
        rows = pl.ds(pl.multiple_of(off, K), K)
        count = sel[0]
        for m in sel[1:]:
            count = count + m
        selsum[rows, :] += count
        acc[rows, :] += dot(jnp.concatenate([m.astype(BF16) for m in sel], axis=1), f)

    def pool_step(late, wait, step, carry):
        rows = []
        for half, blocks in enumerate(step_blocks(step)):
            piece = 2 * late + half
            if wait:
                for s in blocks:
                    mid_copy(piece, s, 0, s).wait_recv()
            rows += [g_mid[s, pl.ds(PIECES[piece][0], 64), :] for s in blocks]
        f = jnp.concatenate(rows, axis=0)
        f = jnp.maximum(dot(f, pool[...]), 0.0).astype(BF16)
        feats[feat_rows(late, step, 1), :] = f
        pool_into(key_off, selector(late, step, key_off), f)
        return carry

    acc[...] = jnp.zeros(acc.shape, F32)
    selsum[...] = jnp.zeros(selsum.shape, F32)
    for late in range(2):
        pool_step(late, False, 0, 0)
        if late == 0:
            onward((2, 3))
        lax.fori_loop(1, 4, functools.partial(pool_step, late, True), 0)
    fetch["tokens"].wait()
    ones = jnp.ones((H, 128), BF16)

    def finish_chunk(first):
        rows = pl.ds(pl.multiple_of(first, 128), 128)
        inv = 1.0 / dot(selsum[rows, :].astype(BF16), ones)
        inv = jnp.concatenate([inv] * (C // 128), axis=1)
        m = (tokens[rows, :].astype(F32) + acc[rows, :] * inv).astype(BF16)
        tmid[rows, :] = m
        tnorm[rows, :] = norm(m.astype(F32)).astype(BF16)

    z0, core0 = (c // 2) // 2, lax.rem(c // 2, 2)
    away = lax.rem(z - z0 + 4, 4)
    on_core = core == core0
    is_src = on_core & (away == 0)
    is_sib = jnp.logical_not(on_core) & (away == 0)
    odd = jnp.where(on_core, 0, 1)
    swap = jnp.where(away == 3, 1, 0)
    up, down = (lax.rem(z + 1, 4) * 2 + core, c), (lax.rem(z + 3, 4) * 2 + core, c)
    onward_id = (lax.rem(z + away, 4) * 2 + core, c)

    def key_copy(q, slot, dev):
        rows = knorm.at[pl.ds(pl.multiple_of(q * OWN, OWN), OWN)]
        return remote(rows, rows, key_s.at[q, slot], key_r.at[q], dev)

    def chip_part(n):
        return 2 * lax.rem(n + 2 * swap, 4) + odd

    for pair in range(2):
        finish_chunk(key_off + 128 * pair)

        @pl.when(is_src)
        def _():
            rows = pl.ds(pl.multiple_of(key_off + 128 * pair, 128), 128)
            knorm[pl.ds(128 * pair, 128), :] = tnorm[rows, :]
            q = 4 * pair
            for p in (q + 1, q + 3):
                key_copy(p, 2, sibling).start()
            for p in (q, q + 2):
                key_copy(p, 0, up).start()
            if pair == 1:
                for p in (4, 6, 0, 2):
                    key_copy(p, 1, down).start()
            for p in (q, q + 2):
                key_copy(p, 2, sibling).start()

    @pl.when(is_sib)
    def _():
        for p in (1, 3, 5, 7):
            key_copy(p, 0, up).wait_recv()
            key_copy(p, 0, up).start()
            if p > 4:
                key_copy(p, 1, down).start()
        for p in (1, 3):
            key_copy(p, 1, down).start()

    other_off = K - key_off

    def other_step(half, step, carry):
        sel = selector(half, 2 * step, other_off) + selector(half, 2 * step + 1, other_off)
        pool_into(other_off, sel, feats[feat_rows(half, 2 * step, 2), :])
        return carry

    for half in range(2):
        lax.fori_loop(0, 2, functools.partial(other_step, half), 0)
    own_rows = pl.ds(pl.multiple_of(c * OWN, OWN), OWN)
    for n in range(4):

        @pl.when(away != 0)
        def _():
            key_copy(chip_part(n), 2, sibling).wait_recv()

        if n < 2:

            @pl.when((away == 1) | (away == 3))
            def _():
                key_copy(chip_part(n), 0, onward_id).start()

        @pl.when(away != 0)
        def _():
            key_copy(chip_part(n), 2, sibling).start()

        if n < 2:
            finish_chunk(other_off + 128 * n)
        else:
            if n == 2:
                fetch["tq"].wait()
            for i in (2 * n - 4, 2 * n - 3):
                q_s[pl.ds(128 * i, 128), :] = dot(tnorm[pl.ds(128 * i, 128), :], tq[...]).astype(BF16)

    @pl.when(jnp.logical_not(is_src))
    def _():
        for n in range(4):
            q = 2 * n + 1 - odd
            key_copy(q, 2, sibling).wait_recv()

    fetch["tkv"].wait()
    kt = (dot(knorm[...], tkv[:, :C]) * (DT**-0.5)).T
    row_i = iota((C, 1), 0)
    v_full = dot(knorm[...], tkv[:, C:])
    lane_i = iota((1, C), 1)
    for g in range(2):
        for h in range(8):
            b0, n = SPANS[h]
            lo, hi = G * g + 128 * b0, G * g + 128 * (b0 + n)
            start = G * g + DT * h
            rm = (row_i[lo:hi] >= start) & (row_i[lo:hi] < start + DT)
            kt_s[8 * g + h, pl.ds(0, 128 * n), :] = jnp.where(rm, kt[lo:hi], 0.0).astype(BF16)
            lm = (lane_i[:, lo:hi] >= start) & (lane_i[:, lo:hi] < start + DT)
            v_s[8 * g + h, :, pl.ds(0, 128 * n)] = jnp.where(lm, v_full[:, lo:hi], 0.0).astype(BF16)
    fetch["tmask"].wait()
    fetch["pbias"].wait()

    def one_copy(g, d):
        return remote(snd.at[g, d], rcv.at[g, lax.rem(c // (1 + 3 * g), 4)], one_s.at[g, d],
                      one_r.at[g, lax.rem(c // (1 + 3 * g), 4)], (r, (y * 4 + d) * (1 - g) + (d * 4 + x) * g))

    def attend(offsets, g, carry):
        me = lax.rem(c // (1 + 3 * g), 4)
        dests = [lax.rem(me + o, 4) for o in offsets]
        size = 128 * len(dests)
        rows = [
            pl.ds(pl.multiple_of((b * (4 - 3 * g) + d * (1 + 3 * g)) * OWN, OWN), OWN) for d in dests for b in range(4)
        ]
        live = tmask[...] == 1
        lane8 = lax.rem(iota((size, 128), 1), 8)
        parts = [None] * 3
        stat = jnp.zeros((size, 128), F32)
        for h in range(8):
            b0, n = SPANS[h]
            lanes = pl.ds(pl.multiple_of(g * G + 128 * b0, 128), 128 * n)
            qw = jnp.concatenate([q_s[rw, lanes] for rw in rows], axis=0)
            s = dot(qw, kt_s[g * 8 + h, pl.ds(0, 128 * n), :])
            s = s + jnp.concatenate([pbias[g * 8 + h, rw, :] for rw in rows], axis=0).astype(F32)
            s = jnp.where(live, s, MASKED)
            top = jnp.max(s, axis=-1, keepdims=True)
            e = jnp.exp(s - top)
            total = jnp.sum(e, axis=-1, keepdims=True)
            o = dot(e.astype(BF16), v_s[g * 8 + h, :, pl.ds(0, 128 * n)]) * (1.0 / total)
            for b in range(n):
                ob = o[:, 128 * b : 128 * (b + 1)]
                parts[b0 + b] = ob if parts[b0 + b] is None else parts[b0 + b] + ob
            stat = jnp.where(lane8 == h, top + jnp.log(total), stat)
        stat = split_lse(stat)
        for n, d in enumerate(dests):
            for b in range(3):
                snd[g, d, pl.ds(128 * b, 128), :] = parts[b][128 * n : 128 * (n + 1)].astype(BF16)
            snd[g, d, pl.ds(G, 32), :] = stat[128 * n : 128 * (n + 1)].T[:32].astype(BF16)

            if offsets[n] != 0:
                one_copy(g, d).start()

        return carry

    for offsets in ((2,), (1, 3), (0,)):
        lax.fori_loop(0, 2, functools.partial(attend, offsets), 0)

    fetch["tg"].wait()
    gate_t = sigmoid(dot(tnorm[own_rows, :], tg[...]))
    mine = (x, y)
    join = join_lse()

    def two_copy(g, d):
        dev = (r, d * 4 + x) if g == 0 else (r, y * 4 + d)
        me = mine[1 - g]
        return remote(snd2.at[g, d], rcv2.at[g, me], two_s.at[g, d], two_r.at[g, me], dev)

    for g in range(2):
        blocks = [snd[g, mine[g]]]
        for i in (2, 3, 1):
            d = lax.rem(mine[g] + i, 4)
            remote(snd.at[g, d], rcv.at[g, d], one_s.at[g, d], one_r.at[g, d], (r, near[g](i))).wait_recv()
            blocks.append(rcv[g, d])
        values = [jnp.concatenate([b[128 * k : 128 * (k + 1)] for k in range(3)], axis=1) for b in blocks]
        lse = [
            lax.dot_general(b[G:], join[:32], (((0,), (0,)), ((), ())), preferred_element_type=F32) for b in blocks
        ]
        half_merged = merge(values, lse, True)
        for d in range(4):
            snd2[g, d] = half_merged[OWN * d : OWN * (d + 1)]
        for i in (2, 1, 3):
            two_copy(g, lax.rem(mine[1 - g] + i, 4)).start()
    merged = []
    for g in range(2):
        blocks = [snd2[g, mine[1 - g]]]
        for i in (1, 3, 2):
            d = lax.rem(mine[1 - g] + i, 4)
            remote(snd2.at[g, d], rcv2.at[g, d], two_s.at[g, d], two_r.at[g, d], (r, near[1 - g](i))).wait_recv()
            blocks.append(rcv2[g, d])
        merged.append(merge([b[:, :G] for b in blocks], [dot(b[:, G:], join) for b in blocks], False))
    att = jnp.concatenate(merged, axis=1)

    for name in ("to", "rg", "ru", "rd"):
        fetch[name].wait()
    gated = (att * gate_t).astype(BF16)
    t_att = (tmid[own_rows, :].astype(F32) + dot(gated, to[...])).astype(BF16)
    n_att = norm(t_att.astype(F32)).astype(BF16)
    up = dot(n_att, rg[...])
    hid = (up * sigmoid(up) * dot(n_att, ru[...])).astype(BF16)
    t_new = (t_att.astype(F32) + dot(hid, rd[...])).astype(BF16)
    g_new[own_rows, :] = t_new

    def rows_of(half, s):
        return pl.ds(pl.multiple_of(s * OWN + 16 * half, 16), 16)

    def new_copy(half, s, slot, dev):
        dst = g_new if slot < 3 else tokens_out
        return remote(
            g_new.at[rows_of(half, s)], dst.at[rows_of(half, s)], new_s.at[half, slot], new_r.at[half, s], (r, dev)
        )

    out_copies = [pltpu.make_async_copy(g_new.at[own_rows], tokens_out.at[own_rows], own_sem.at[4])]
    def new_start(half, s, slot, dev):
        new_copy(half, s, slot, dev).start()

    for half in range(2):
        own_hops(half, new_start)
    out_copies[0].start()
    for half in range(2):
        for k, i in enumerate((1, 3, 2)):
            rows = rows_of(half, near[half](i))
            out_copies.append(pltpu.make_async_copy(g_new.at[rows], tokens_out.at[rows], own_sem.at[5 + 3 * half + k]))

    for k in range(3):
        for half in range(2):
            next_hops(half, k, new_copy, new_start)
    for cp in out_copies[1:]:
        cp.start()

    for half in range(2):
        for i in (1, 3, 2):
            for j in range(4):
                s = y_peer(i) // 4 * 4 + j if half == 0 else j * 4 + lax.rem(x + i, 4)
                new_copy(half, s, 3, s).wait_recv()
    for cp in mid_out_copies + out_copies:
        cp.wait()
    for cp in halo:
        cp.wait_send()

    for piece in range(4):
        all_hops(piece, lambda *a: mid_copy(*a).wait_send())
    for half in range(2):
        all_hops(half, lambda *a: new_copy(*a).wait_send())
    for g in range(2):
        for i in (1, 3, 2):
            one_copy(g, lax.rem(mine[g] + i, 4)).wait_send()
            two_copy(g, lax.rem(mine[1 - g] + i, 4)).wait_send()

    @pl.when(is_src)
    def _():
        for q in range(8):
            key_copy(q, 2, sibling).wait_send()
            if q % 2 == 0:
                key_copy(q, 0, up).wait_send()
                key_copy(q, 1, down).wait_send()

    @pl.when(is_sib)
    def _():
        for q in (1, 3, 5, 7):
            key_copy(q, 0, up).wait_send()
            key_copy(q, 1, down).wait_send()

    @pl.when(away != 0)
    def _():
        for n in range(4):
            key_copy(chip_part(n), 2, sibling).wait_send()

    @pl.when((away == 1) | (away == 3))
    def _():
        for n in (0, 1):
            key_copy(chip_part(n), 0, onward_id).wait_send()


def to_atoms(mid, new, back, atok, atoms_out, tokens_out, mid_v, new_v, back_v, atok_v, in_sem, out_sem):
    n = 8
    rows = [pl.ds(i * (T // n), T // n) for i in range(n)]
    ins = [pltpu.make_async_copy(new.at[w], new_v.at[w], in_sem.at[i]) for i, w in enumerate(rows)]
    small = [
        pltpu.make_async_copy(a, b, in_sem.at[n + i])
        for i, (a, b) in enumerate(((atok, atok_v), (back, back_v), (mid, mid_v)))
    ]
    outs = [pltpu.make_async_copy(new_v.at[w], tokens_out.at[w], out_sem.at[i]) for i, w in enumerate(rows)]
    for cp in ins[:2] + small + ins[2:]:
        cp.start()
    first = lax.axis_index("row") * T
    lane = iota((A, 128), 1).astype(F32)
    ins[0].wait()
    outs[0].start()
    for cp in small:
        cp.wait()
    tok_t = jnp.broadcast_to((atok_v[...] - first).astype(F32), (128, A)).T
    update = None
    for i, w in enumerate(rows):
        if i > 0:
            ins[i].wait()
            outs[i].start()
        if i % 2 == 1:
            w = pl.ds(T // n * (i - 1), 128)
            pick = jnp.where(tok_t == lane + float(T // n * (i - 1)), 1.0, 0.0).astype(BF16)
            term = dot(pick, dot(new_v[w, :], back_v[...]).astype(BF16))
            update = term if update is None else update + term
    mid_v[...] = (mid_v[...].astype(F32) + update).astype(BF16)
    last = pltpu.make_async_copy(mid_v, atoms_out, out_sem.at[n])
    last.start()
    for cp in outs + [last]:
        cp.wait()


def on_device(
    atoms, atom_bias, key_mask, atom_token, tokens, pair_bias, token_mask,
    atom_query, atom_keyval, atom_gate, atom_out, pool_weight,
    token_query, token_keyval, token_gate, token_out, trans_gate, trans_up, trans_down, back_weight,
):
    atok = atom_token.reshape(1, A)
    args = (
        atoms, atom_bias.reshape(A * HA, WK), key_mask, atok, tokens, pair_bias,
        token_mask.reshape(1, K), atom_query, atom_keyval, atom_gate, atom_out, pool_weight,
        token_query, token_keyval, token_gate, token_out, trans_gate, trans_up, trans_down,
    )
    vmem = [pltpu.VMEM(a.shape, a.dtype) for a in args]
    vmem[0] = pltpu.VMEM((A + 2 * REACH, 128), BF16)
    dma = pltpu.SemaphoreType.DMA
    scratch = vmem + [
        pltpu.VMEM((COLS, A + 32, 128), BF16),
        pltpu.VMEM((COLS * A, C), BF16),
        pltpu.VMEM((T, C), F32),
        pltpu.VMEM((T, H), F32),
        pltpu.VMEM((T, C), BF16),
        pltpu.VMEM((T, C), BF16),
        pltpu.VMEM((K, C), BF16),
        pltpu.VMEM((T, C), BF16),
        pltpu.VMEM((16, 256, K), BF16),
        pltpu.VMEM((16, K, 256), BF16),
        pltpu.VMEM((2, 4, G + 32, 128), BF16),
        pltpu.VMEM((2, 4, G + 32, 128), BF16),
        pltpu.VMEM((2, 4, OWN, G + 128), BF16),
        pltpu.VMEM((2, 4, OWN, G + 128), BF16),
        pltpu.VMEM((T, C), BF16),
        dma((len(args),)), dma((2,)), dma((2,)),
        dma((4, COLS)), dma((4, COLS)),
        dma((8, 3)), dma((8,)),
        dma((2, 4)), dma((2, 4)), dma((2, 4)), dma((2, 4)),
        dma((2, COLS)), dma((2, COLS)), dma((11,)),
    ]
    mid, new = pl.pallas_call(
        kernel,
        out_shape=(jax.ShapeDtypeStruct((A, 128), BF16), jax.ShapeDtypeStruct((T, C), BF16)),
        in_specs=[pl.BlockSpec(memory_space=pl.ANY)] * len(args),
        out_specs=(pl.BlockSpec(memory_space=pl.ANY),) * 2,
        scratch_shapes=scratch,
        compiler_params=pltpu.CompilerParams(
            collective_id=0, has_side_effects=True, vmem_limit_bytes=60 * 1024 * 1024
        ),
        name="block",
    )(*args)
    hbm = pl.BlockSpec(memory_space=pl.ANY)
    return pl.pallas_call(
        to_atoms,
        out_shape=(jax.ShapeDtypeStruct((A, 128), BF16), jax.ShapeDtypeStruct((T, C), BF16)),
        in_specs=[hbm] * 4,
        out_specs=(hbm, hbm),
        scratch_shapes=[
            pltpu.VMEM((A, 128), BF16), pltpu.VMEM((T, C), BF16), pltpu.VMEM((C, 128), BF16), pltpu.VMEM((1, A), jnp.int32),
            dma((11,)), dma((9,)),
        ],
        compiler_params=pltpu.CompilerParams(vmem_limit_bytes=60 * 1024 * 1024),
        name="to_atoms",
    )(mid, new, back_weight, atok)


def solution(mesh):
    both = ("row", "col")
    in_specs = (
        P(both, None), P(both, None, None), P(both, None), P(both), P("row", None), P(None, "row", "col"), P("col"),
    ) + (P(),) * 13
    out_specs = (P(both, None), P("row", None))
    return jax.shard_map(on_device, mesh=mesh, in_specs=in_specs, out_specs=out_specs, check_vma=False)
```

```python
import functools

import jax
import jax.numpy as jnp
from jax import lax
from jax.experimental import pallas as pl
from jax.experimental.pallas import tpu as pltpu
from jax.sharding import PartitionSpec as P

F32 = jnp.float32
BF16 = jnp.bfloat16
MESH = pl.DeviceIdType.MESH
ROWS, COLS = 8, 16
EPSILON = 1e-05
MASKED = -1000000000.0
HA, DA, WQ, WK = 4, 32, 32, 128
DT = 48
REACH = 48
A = 256
T = 512
PIECES = ((0, 80), (80, 80), (160, 64), (224, 64))
K = 256
C = 768
G = 384
OWN = 32
H = 128
TOTAL_ATOMS = 32768


def dot(a, b):
    return jnp.dot(a, b, preferred_element_type=F32)


def norm(x):
    mean = jnp.mean(x, axis=-1, keepdims=True)
    d = x - mean
    var = jnp.mean(d * d, axis=-1, keepdims=True)
    return d * lax.rsqrt(var + EPSILON)


def sigmoid(x):
    return 1.0 / (1.0 + jnp.exp(-x))


def iota(shape, dim):
    return lax.broadcasted_iota(jnp.int32, shape, dim)


IN_NAMES = (
    "atoms", "abias", "kmask", "atok", "tokens", "pbias", "tmask", "aq", "akv", "ag", "ao", "pool",
    "tq", "tkv", "tg", "to", "rg", "ru", "rd",
)
EARLY = ("atoms", "akv", "aq", "ag", "kmask", "abias", "ao", "atok", "pool")
LATE = ("tokens", "tg", "tq", "tkv", "tmask", "pbias", "to", "rg", "ru", "rd")
SPANS = tuple(((DT * h) // 128, (DT * h + DT - 1) // 128 - (DT * h) // 128 + 1) for h in range(8))


def split_lse(stat):
    high = stat.astype(BF16).astype(F32)
    rest = stat - high
    middle = rest.astype(BF16).astype(F32)
    third = iota(stat.shape, 1) // 8
    return jnp.where(third == 0, high, jnp.where(third == 1, middle, rest - middle))


def join_lse():
    l_r, l_c = iota((128, 128), 0), iota((128, 128), 1)
    return jnp.where((l_r < 24) & (lax.rem(l_r, 8) == lax.rem(l_c, 8)), 1.0, 0.0).astype(BF16)


def merge(values, lse, want_lse):
    s_r, s_c = iota((128, G), 0), iota((128, G), 1)
    spread = jnp.where((s_r < 16) & (lax.rem(s_r, 8) == s_c // DT), 1.0, 0.0).astype(BF16)
    top = lse[0]
    for l in lse[1:]:
        top = jnp.maximum(top, l)
    wgt = [jnp.exp(l - top) for l in lse]
    total = wgt[0]
    for w in wgt[1:]:
        total = total + w
    inv = 1.0 / total
    first = iota(top.shape, 1) < 8
    out = None
    for w, v in zip(wgt, values):
        w = w * inv
        high = w.astype(BF16).astype(F32)
        term = dot(jnp.where(first, high, w - high).astype(BF16), spread) * v.astype(F32)
        out = term if out is None else out + term
    if want_lse:
        return jnp.concatenate([out, split_lse(top + jnp.log(total))], axis=1).astype(BF16)
    return out


def kernel(*refs):
    n_in = len(IN_NAMES)
    hbm = dict(zip(IN_NAMES, refs[:n_in]))
    mid_out, tokens_out = refs[n_in : n_in + 2]
    (
        ext, abias, kmask, tk, tokens, pbias, tmask, aq, akv, ag, ao, pool, tq, tkv, tg, to, rg, ru, rd,
        g_mid, feats, acc, selsum, tmid, tnorm, knorm, q_s, kt_s, v_s, snd, rcv, snd2, rcv2, g_new,
        in_sem, halo_s, halo_r, mid_s, mid_r, key_s, key_r,
        one_s, one_r, two_s, two_r, new_s, new_r, own_sem,
    ) = refs[n_in + 2 :]

    r = lax.axis_index("row")
    c = lax.axis_index("col")
    y, x = c // 4, lax.rem(c, 4)
    z, core = r // 2, lax.rem(r, 2)
    lin = r * COLS + c
    nxt = lax.rem(lin + 1, ROWS * COLS)
    prv = lax.rem(lin + ROWS * COLS - 1, ROWS * COLS)
    nxt_id = (nxt // COLS, lax.rem(nxt, COLS))
    prv_id = (prv // COLS, lax.rem(prv, COLS))
    sibling = (z * 2 + 1 - core, c)

    def remote(src, dst, ss, rs, dev):
        return pltpu.make_async_remote_copy(
            src_ref=src, dst_ref=dst, send_sem=ss, recv_sem=rs, device_id=dev, device_id_type=MESH
        )

    def x_peer(i):
        return y * 4 + lax.rem(x + i, 4)

    def y_peer(i):
        return lax.rem(y + i, 4) * 4 + x

    near = (x_peer, y_peer)

    bar = pltpu.get_barrier_semaphore()
    partners = [nxt_id, prv_id, (lax.rem(z + 1, 4) * 2 + core, c), (lax.rem(z + 3, 4) * 2 + core, c)]
    partners += [(r, peer(i)) for i in (2, 1, 3) for peer in near] + [sibling]
    for dev in partners:
        pl.semaphore_signal(bar, inc=1, device_id=dev, device_id_type=MESH)

    fetch = {}
    vm = dict(
        atoms=ext.at[pl.ds(REACH, A)], abias=abias, kmask=kmask, atok=tk, tokens=tokens, pbias=pbias, tmask=tmask,
        aq=aq, akv=akv, ag=ag, ao=ao, pool=pool, tq=tq, tkv=tkv, tg=tg, to=to, rg=rg, ru=ru, rd=rd,
    )
    for i, name in enumerate(EARLY + LATE):
        fetch[name] = pltpu.make_async_copy(hbm[name], vm[name], in_sem.at[i])
    for name in EARLY:
        fetch[name].start()

    for name in ("atoms", "akv", "aq", "ag"):
        fetch[name].wait()
    own_f = ext[pl.ds(REACH, A), :].astype(F32)
    own_n = norm(own_f).astype(BF16)
    q_a = dot(own_n, aq[...]).astype(BF16)
    gate_a = sigmoid(dot(own_n, ag[...]))
    kv_own = dot(own_n, akv[...]).astype(BF16)
    fetch["kmask"].wait()
    fetch["abias"].wait()
    p_r = iota((HA * WQ, HA * WQ), 0)
    p_c = iota((HA * WQ, HA * WQ), 1)
    perm = (p_c == lax.rem(p_r, WQ) * HA + p_r // WQ).astype(F32).astype(BF16)
    bias_w = [dot(perm, abias[pl.ds(HA * WQ * w, HA * WQ), :]) for w in range(A // WQ)]
    lane = iota((1, WK), 1)
    head_f = [jnp.where((lane // DA) == h, 1.0, 0.0).astype(F32) for h in range(HA)]
    head_b = [f.astype(BF16) for f in head_f]

    def window(w, kv):
        q_w = q_a[WQ * w : WQ * (w + 1)]
        q_bd = jnp.concatenate([q_w * head_b[h] for h in range(HA)], axis=0)
        s = lax.dot_general(q_bd, kv[:, :WK], (((1,), (1,)), ((), ())), preferred_element_type=F32)
        s = s * (DA**-0.5) + bias_w[w]
        pos = lin * A + WQ * w + lane - REACH
        valid = (kmask[pl.ds(w, 1), :] == 1) & (pos >= 0) & (pos < TOTAL_ATOMS)
        s = jnp.where(valid, s, MASKED)
        e = jnp.exp(s - jnp.max(s, axis=-1, keepdims=True))
        t = jnp.sum(e, axis=-1, keepdims=True)
        o = dot(e.astype(BF16), kv[:, WK:]) / t
        return sum(o[WQ * h : WQ * (h + 1)] * head_f[h] for h in range(HA))

    def mid_of(first, attended):
        rows = slice(first, first + WQ * len(attended))
        gated = (jnp.concatenate(attended, axis=0) * gate_a[rows]).astype(BF16)
        return (own_f[rows] + dot(gated, ao[...])).astype(BF16)

    def put(piece, rows):
        g_mid[c, PIECES[piece][0] : PIECES[piece][0] + 64, :] = rows

    fetch["ao"].wait()
    inner = mid_of(64, [window(w, kv_own[WQ * w - REACH : WQ * w - REACH + WK]) for w in (2, 3, 4, 5)])
    put(0, inner[:64])
    put(1, inner[64:])
    fetch["atok"].wait()
    numbers = jnp.broadcast_to(tk[...] - r * T, (16, A))
    turned, rest = pltpu.roll(numbers[:, :H], 64, 1), numbers[:, H:]
    left = iota((16, H), 1) < 64
    line = iota((16, H), 0)
    for piece in range(2):
        number = jnp.where(left, turned, rest) if piece == 0 else jnp.where(left, rest, turned)
        number = jnp.where(line == 0, number >> 1, jnp.where(line == 1, number & 1, 0))
        g_mid[c, 64 + 80 * piece : 80 + 80 * piece, :] = number.astype(F32).astype(BF16)
    pl.semaphore_wait(bar, len(partners))

    halo = [
        remote(ext.at[pl.ds(A, REACH)], ext.at[pl.ds(0, REACH)], halo_s.at[0], halo_r.at[0], nxt_id),
        remote(ext.at[pl.ds(REACH, REACH)], ext.at[pl.ds(REACH + A, REACH)], halo_s.at[1], halo_r.at[1], prv_id),
    ]
    for cp in halo:
        cp.start()

    def mid_copy(piece, s, slot, dev):
        rows = g_mid.at[s, pl.ds(*PIECES[piece])]
        return remote(rows, rows, mid_s.at[piece, slot], mid_r.at[piece, s], (r, dev))

    def own_hops(piece, send):
        half = piece % 2
        for i in (2, 1, 3):
            send(piece, c, i - 1, near[half](i))
        for i in (2, 1, 3):
            send(piece, c, i + 2, near[1 - half](i))

    def next_hops(piece, k, wait, send):
        half = piece % 2
        s = near[half]((1, 3, 2)[k])
        if wait is not None:
            wait(piece, s, 0, c).wait_recv()
        for i in (2, 1, 3):
            send(piece, s, 3 * k + i + 5, near[1 - half](i))

    def all_hops(piece, send):
        own_hops(piece, send)
        for k in range(3):
            next_hops(piece, k, None, send)

    def mid_start(piece, s, slot, dev):
        mid_copy(piece, s, slot, dev).start()

    def onward(pieces):
        for k in range(3):
            for piece in pieces:
                next_hops(piece, k, mid_copy, mid_start)

    own_hops(0, mid_start)
    own_hops(1, mid_start)
    for name in LATE:
        fetch[name].start()
    onward((0, 1))
    edges = []
    for side in range(2):
        halo[side].wait_recv()
        edge = norm(ext[pl.ds((REACH + A) * side, REACH), :].astype(F32)).astype(BF16)
        inside = jnp.where(lin == (ROWS * COLS - 1) * side, 0.0, 1.0).astype(F32)
        edges.append((dot(edge, akv[...]) * inside).astype(BF16))
    near_by = jnp.concatenate([kv_own[6 * WQ - REACH :], edges[1]], axis=0)
    put(2, mid_of(192, [window(6, near_by[:WK]), window(7, near_by[WQ : WQ + WK])]))
    own_hops(2, mid_start)
    near_by = jnp.concatenate([edges[0], kv_own[: WK - WQ + 16]], axis=0)
    put(3, mid_of(0, [window(0, near_by[:WK]), window(1, near_by[WQ : WQ + WK])]))
    own_hops(3, mid_start)
    mid_out_copies = [
        pltpu.make_async_copy(g_mid.at[c, pl.ds(PIECES[i][0], 64)], mid_out.at[pl.ds(b, 64)], own_sem.at[i])
        for i, b in enumerate((64, 128, 192, 0))
    ]
    for cp in mid_out_copies:
        cp.start()

    fetch["pool"].wait()

    key_off = lax.rem(c, 2) * K

    def step_blocks(step):
        o = lax.rem(step * (step + 1) // 2, 4)
        return [lax.rem(y + o, 4) * 4 + b for b in range(4)], [b * 4 + lax.rem(x + o, 4) for b in range(4)]

    def selector(late, step, off):
        at = (iota((K, H), 0) + off).astype(F32)
        left = iota((8, H), 1) < 64
        sel = []
        for half, blocks in enumerate(step_blocks(step)):
            numbers = []
            for s in blocks:
                terms = g_mid[s, 64 + 80 * half : 80 + 80 * half, :].astype(F32)
                numbers.append(jnp.broadcast_to(2.0 * terms[0:1] + terms[1:2], (8, H)))
            for n in (0, 2):
                if late:
                    pair = jnp.where(left, pltpu.roll(numbers[n], 64, 1), numbers[n + 1])
                else:
                    pair = jnp.where(left, numbers[n], pltpu.roll(numbers[n + 1], 64, 1))
                sel.append(jnp.where(at == pair[0:1], 1.0, 0.0).astype(F32))
        return sel

    def feat_rows(half, step, n):
        return pl.ds(pl.multiple_of((4 * half + step) * 512, 512), 512 * n)

    def pool_into(off, sel, f):
        rows = pl.ds(pl.multiple_of(off, K), K)
        count = sel[0]
        for m in sel[1:]:
            count = count + m
        selsum[rows, :] += count
        acc[rows, :] += dot(jnp.concatenate([m.astype(BF16) for m in sel], axis=1), f)

    def pool_step(late, wait, step, carry):
        rows = []
        for half, blocks in enumerate(step_blocks(step)):
            piece = 2 * late + half
            if wait:
                for s in blocks:
                    mid_copy(piece, s, 0, s).wait_recv()
            rows += [g_mid[s, pl.ds(PIECES[piece][0], 64), :] for s in blocks]
        f = jnp.concatenate(rows, axis=0)
        f = jnp.maximum(dot(f, pool[...]), 0.0).astype(BF16)
        feats[feat_rows(late, step, 1), :] = f
        pool_into(key_off, selector(late, step, key_off), f)
        return carry

    acc[...] = jnp.zeros(acc.shape, F32)
    selsum[...] = jnp.zeros(selsum.shape, F32)
    for late in range(2):
        pool_step(late, False, 0, 0)
        if late == 0:
            onward((2, 3))
        lax.fori_loop(1, 4, functools.partial(pool_step, late, True), 0)
    fetch["tokens"].wait()
    ones = jnp.ones((H, 128), BF16)

    def finish_chunk(first):
        rows = pl.ds(pl.multiple_of(first, 128), 128)
        inv = 1.0 / dot(selsum[rows, :].astype(BF16), ones)
        inv = jnp.concatenate([inv] * (C // 128), axis=1)
        m = (tokens[rows, :].astype(F32) + acc[rows, :] * inv).astype(BF16)
        tmid[rows, :] = m
        tnorm[rows, :] = norm(m.astype(F32)).astype(BF16)

    z0, core0 = (c // 2) // 2, lax.rem(c // 2, 2)
    away = lax.rem(z - z0 + 4, 4)
    on_core = core == core0
    is_src = on_core & (away == 0)
    is_sib = jnp.logical_not(on_core) & (away == 0)
    odd = jnp.where(on_core, 0, 1)
    swap = jnp.where(away == 3, 1, 0)
    up, down = (lax.rem(z + 1, 4) * 2 + core, c), (lax.rem(z + 3, 4) * 2 + core, c)
    onward_id = (lax.rem(z + away, 4) * 2 + core, c)

    def key_copy(q, slot, dev):
        rows = knorm.at[pl.ds(pl.multiple_of(q * OWN, OWN), OWN)]
        return remote(rows, rows, key_s.at[q, slot], key_r.at[q], dev)

    def chip_part(n):
        return 2 * lax.rem(n + 2 * swap, 4) + odd

    for pair in range(2):
        finish_chunk(key_off + 128 * pair)

        @pl.when(is_src)
        def _():
            rows = pl.ds(pl.multiple_of(key_off + 128 * pair, 128), 128)
            knorm[pl.ds(128 * pair, 128), :] = tnorm[rows, :]
            q = 4 * pair
            for p in (q + 1, q + 3):
                key_copy(p, 2, sibling).start()
            for p in (q, q + 2):
                key_copy(p, 0, up).start()
            if pair == 1:
                for p in (4, 6, 0, 2):
                    key_copy(p, 1, down).start()
            for p in (q, q + 2):
                key_copy(p, 2, sibling).start()

    @pl.when(is_sib)
    def _():
        for p in (1, 3, 5, 7):
            key_copy(p, 0, up).wait_recv()
            key_copy(p, 0, up).start()
            if p > 4:
                key_copy(p, 1, down).start()
        for p in (1, 3):
            key_copy(p, 1, down).start()

    other_off = K - key_off

    def other_step(half, step, carry):
        sel = selector(half, 2 * step, other_off) + selector(half, 2 * step + 1, other_off)
        pool_into(other_off, sel, feats[feat_rows(half, 2 * step, 2), :])
        return carry

    for half in range(2):
        lax.fori_loop(0, 2, functools.partial(other_step, half), 0)
    own_rows = pl.ds(pl.multiple_of(c * OWN, OWN), OWN)
    fetch["tq"].wait()

    def queries():
        for i in range(4):
            rows = pl.ds(128 * i, 128)
            q_s[rows, :] = dot(tnorm[rows, :], tq[...]).astype(BF16)

    between = [lambda: finish_chunk(other_off), lambda: finish_chunk(other_off + 128), queries]

    @pl.when(away == 2)
    def _():
        for work in between:
            work()

    for n in range(4):

        @pl.when(away != 0)
        def _():
            key_copy(chip_part(n), 2, sibling).wait_recv()

        if n < 2:

            @pl.when((away == 1) | (away == 3))
            def _():
                key_copy(chip_part(n), 0, onward_id).start()

        @pl.when(away != 0)
        def _():
            key_copy(chip_part(n), 2, sibling).start()

        if n < 3:
            pl.when(away != 2)(between[n])

    @pl.when(jnp.logical_not(is_src))
    def _():
        for n in range(4):
            q = 2 * n + 1 - odd
            key_copy(q, 2, sibling).wait_recv()

    fetch["tkv"].wait()
    kt = (dot(knorm[...], tkv[:, :C]) * (DT**-0.5)).T
    row_i = iota((C, 1), 0)
    v_full = dot(knorm[...], tkv[:, C:])
    lane_i = iota((1, C), 1)
    for g in range(2):
        for h in range(8):
            b0, n = SPANS[h]
            lo, hi = G * g + 128 * b0, G * g + 128 * (b0 + n)
            start = G * g + DT * h
            rm = (row_i[lo:hi] >= start) & (row_i[lo:hi] < start + DT)
            kt_s[8 * g + h, pl.ds(0, 128 * n), :] = jnp.where(rm, kt[lo:hi], 0.0).astype(BF16)
            lm = (lane_i[:, lo:hi] >= start) & (lane_i[:, lo:hi] < start + DT)
            v_s[8 * g + h, :, pl.ds(0, 128 * n)] = jnp.where(lm, v_full[:, lo:hi], 0.0).astype(BF16)
    fetch["tmask"].wait()
    fetch["pbias"].wait()

    def one_copy(g, d):
        return remote(snd.at[g, d], rcv.at[g, lax.rem(c // (1 + 3 * g), 4)], one_s.at[g, d],
                      one_r.at[g, lax.rem(c // (1 + 3 * g), 4)], (r, (y * 4 + d) * (1 - g) + (d * 4 + x) * g))

    def attend(offsets, g, carry):
        me = lax.rem(c // (1 + 3 * g), 4)
        dests = [lax.rem(me + o, 4) for o in offsets]
        size = 128 * len(dests)
        rows = [
            pl.ds(pl.multiple_of((b * (4 - 3 * g) + d * (1 + 3 * g)) * OWN, OWN), OWN) for d in dests for b in range(4)
        ]
        live = tmask[...] == 1
        lane8 = lax.rem(iota((size, 128), 1), 8)
        parts = [None] * 3
        stat = jnp.zeros((size, 128), F32)
        for h in range(8):
            b0, n = SPANS[h]
            lanes = pl.ds(pl.multiple_of(g * G + 128 * b0, 128), 128 * n)
            qw = jnp.concatenate([q_s[rw, lanes] for rw in rows], axis=0)
            s = dot(qw, kt_s[g * 8 + h, pl.ds(0, 128 * n), :])
            s = s + jnp.concatenate([pbias[g * 8 + h, rw, :] for rw in rows], axis=0).astype(F32)
            s = jnp.where(live, s, MASKED)
            top = jnp.max(s, axis=-1, keepdims=True)
            e = jnp.exp(s - top)
            total = jnp.sum(e, axis=-1, keepdims=True)
            o = dot(e.astype(BF16), v_s[g * 8 + h, :, pl.ds(0, 128 * n)]) * (1.0 / total)
            for b in range(n):
                ob = o[:, 128 * b : 128 * (b + 1)]
                parts[b0 + b] = ob if parts[b0 + b] is None else parts[b0 + b] + ob
            stat = jnp.where(lane8 == h, top + jnp.log(total), stat)
        stat = split_lse(stat)
        for n, d in enumerate(dests):
            for b in range(3):
                snd[g, d, pl.ds(128 * b, 128), :] = parts[b][128 * n : 128 * (n + 1)].astype(BF16)
            snd[g, d, pl.ds(G, 32), :] = stat[128 * n : 128 * (n + 1)].T[:32].astype(BF16)

            if offsets[n] != 0:
                one_copy(g, d).start()

        return carry

    for offsets in ((2,), (1, 3), (0,)):
        lax.fori_loop(0, 2, functools.partial(attend, offsets), 0)

    fetch["tg"].wait()
    gate_t = sigmoid(dot(tnorm[own_rows, :], tg[...]))
    mine = (x, y)
    join = join_lse()

    def two_copy(g, d):
        dev = (r, d * 4 + x) if g == 0 else (r, y * 4 + d)
        me = mine[1 - g]
        return remote(snd2.at[g, d], rcv2.at[g, me], two_s.at[g, d], two_r.at[g, me], dev)

    for g in range(2):
        blocks = [snd[g, mine[g]]]
        for i in (2, 3, 1):
            d = lax.rem(mine[g] + i, 4)
            remote(snd.at[g, d], rcv.at[g, d], one_s.at[g, d], one_r.at[g, d], (r, near[g](i))).wait_recv()
            blocks.append(rcv[g, d])
        values = [jnp.concatenate([b[128 * k : 128 * (k + 1)] for k in range(3)], axis=1) for b in blocks]
        lse = [
            lax.dot_general(b[G:], join[:32], (((0,), (0,)), ((), ())), preferred_element_type=F32) for b in blocks
        ]
        half_merged = merge(values, lse, True)
        for d in range(4):
            snd2[g, d] = half_merged[OWN * d : OWN * (d + 1)]
        for i in (2, 1, 3):
            two_copy(g, lax.rem(mine[1 - g] + i, 4)).start()
    merged = []
    for g in range(2):
        blocks = [snd2[g, mine[1 - g]]]
        for i in (1, 3, 2):
            d = lax.rem(mine[1 - g] + i, 4)
            remote(snd2.at[g, d], rcv2.at[g, d], two_s.at[g, d], two_r.at[g, d], (r, near[1 - g](i))).wait_recv()
            blocks.append(rcv2[g, d])
        merged.append(merge([b[:, :G] for b in blocks], [dot(b[:, G:], join) for b in blocks], False))
    att = jnp.concatenate(merged, axis=1)

    for name in ("to", "rg", "ru", "rd"):
        fetch[name].wait()
    gated = (att * gate_t).astype(BF16)
    t_att = (tmid[own_rows, :].astype(F32) + dot(gated, to[...])).astype(BF16)
    n_att = norm(t_att.astype(F32)).astype(BF16)
    up = dot(n_att, rg[...])
    hid = (up * sigmoid(up) * dot(n_att, ru[...])).astype(BF16)
    t_new = (t_att.astype(F32) + dot(hid, rd[...])).astype(BF16)
    g_new[own_rows, :] = t_new

    def rows_of(half, s):
        return pl.ds(pl.multiple_of(s * OWN + 16 * half, 16), 16)

    def new_copy(half, s, slot, dev):
        dst = g_new if slot < 3 else tokens_out
        return remote(
            g_new.at[rows_of(half, s)], dst.at[rows_of(half, s)], new_s.at[half, slot], new_r.at[half, s], (r, dev)
        )

    out_copies = [pltpu.make_async_copy(g_new.at[own_rows], tokens_out.at[own_rows], own_sem.at[4])]
    def new_start(half, s, slot, dev):
        new_copy(half, s, slot, dev).start()

    for half in range(2):
        own_hops(half, new_start)
    out_copies[0].start()
    for half in range(2):
        for k, i in enumerate((1, 3, 2)):
            rows = rows_of(half, near[half](i))
            out_copies.append(pltpu.make_async_copy(g_new.at[rows], tokens_out.at[rows], own_sem.at[5 + 3 * half + k]))

    for k in range(3):
        for half in range(2):
            next_hops(half, k, new_copy, new_start)
    for cp in out_copies[1:]:
        cp.start()

    for cp in halo:
        cp.wait_send()

    for piece in range(4):
        all_hops(piece, lambda *a: mid_copy(*a).wait_send())
    for g in range(2):
        for i in (1, 3, 2):
            one_copy(g, lax.rem(mine[g] + i, 4)).wait_send()
            two_copy(g, lax.rem(mine[1 - g] + i, 4)).wait_send()

    @pl.when(is_src)
    def _():
        for q in range(8):
            key_copy(q, 2, sibling).wait_send()
            if q % 2 == 0:
                key_copy(q, 0, up).wait_send()
                key_copy(q, 1, down).wait_send()

    @pl.when(is_sib)
    def _():
        for q in (1, 3, 5, 7):
            key_copy(q, 0, up).wait_send()
            key_copy(q, 1, down).wait_send()

    @pl.when(away != 0)
    def _():
        for n in range(4):
            key_copy(chip_part(n), 2, sibling).wait_send()

    @pl.when((away == 1) | (away == 3))
    def _():
        for n in (0, 1):
            key_copy(chip_part(n), 0, onward_id).wait_send()

    for half in range(2):
        for i in (1, 3, 2):
            for j in range(4):
                s = y_peer(i) // 4 * 4 + j if half == 0 else j * 4 + lax.rem(x + i, 4)
                new_copy(half, s, 3, s).wait_recv()
    for cp in mid_out_copies + out_copies:
        cp.wait()
    for half in range(2):
        all_hops(half, lambda *a: new_copy(*a).wait_send())


def to_atoms(mid, new, back, atok, atoms_out, tokens_out, mid_v, new_v, back_v, atok_v, in_sem, out_sem):
    n = 2
    rows = [pl.ds(i * (T // n), T // n) for i in range(n)]
    ins = [pltpu.make_async_copy(new.at[w], new_v.at[w], in_sem.at[i]) for i, w in enumerate(rows)]
    small = [
        pltpu.make_async_copy(a, b, in_sem.at[n + i])
        for i, (a, b) in enumerate(((atok, atok_v), (back, back_v), (mid, mid_v)))
    ]
    outs = [pltpu.make_async_copy(new_v.at[w], tokens_out.at[w], out_sem.at[i]) for i, w in enumerate(rows)]
    for cp in ins[:1] + small + ins[1:]:
        cp.start()
    first = lax.axis_index("row") * T
    lane = iota((A, 128), 1).astype(F32)
    ins[0].wait()
    outs[0].start()
    for cp in small:
        cp.wait()
    tok_t = jnp.broadcast_to((atok_v[...] - first).astype(F32), (128, A)).T
    update = None
    for i, w in enumerate(rows):
        if i > 0:
            ins[i].wait()
            outs[i].start()
        for at in range(T // n * i, T // n * (i + 1), 128):
            pick = jnp.where(tok_t == lane + float(at), 1.0, 0.0).astype(BF16)
            term = dot(pick, dot(new_v[pl.ds(at, 128), :], back_v[...]).astype(BF16))
            update = term if update is None else update + term
    mid_v[...] = (mid_v[...].astype(F32) + update).astype(BF16)
    last = pltpu.make_async_copy(mid_v, atoms_out, out_sem.at[n])
    last.start()
    for cp in outs + [last]:
        cp.wait()


def on_device(
    atoms, atom_bias, key_mask, atom_token, tokens, pair_bias, token_mask,
    atom_query, atom_keyval, atom_gate, atom_out, pool_weight,
    token_query, token_keyval, token_gate, token_out, trans_gate, trans_up, trans_down, back_weight,
):
    atok = atom_token.reshape(1, A)
    args = (
        atoms, atom_bias.reshape(A * HA, WK), key_mask, atok, tokens, pair_bias,
        token_mask.reshape(1, K), atom_query, atom_keyval, atom_gate, atom_out, pool_weight,
        token_query, token_keyval, token_gate, token_out, trans_gate, trans_up, trans_down,
    )
    vmem = [pltpu.VMEM(a.shape, a.dtype) for a in args]
    vmem[0] = pltpu.VMEM((A + 2 * REACH, 128), BF16)
    dma = pltpu.SemaphoreType.DMA
    scratch = vmem + [
        pltpu.VMEM((COLS, A + 32, 128), BF16),
        pltpu.VMEM((COLS * A, C), BF16),
        pltpu.VMEM((T, C), F32),
        pltpu.VMEM((T, H), F32),
        pltpu.VMEM((T, C), BF16),
        pltpu.VMEM((T, C), BF16),
        pltpu.VMEM((K, C), BF16),
        pltpu.VMEM((T, C), BF16),
        pltpu.VMEM((16, 256, K), BF16),
        pltpu.VMEM((16, K, 256), BF16),
        pltpu.VMEM((2, 4, G + 32, 128), BF16),
        pltpu.VMEM((2, 4, G + 32, 128), BF16),
        pltpu.VMEM((2, 4, OWN, G + 128), BF16),
        pltpu.VMEM((2, 4, OWN, G + 128), BF16),
        pltpu.VMEM((T, C), BF16),
        dma((len(args),)), dma((2,)), dma((2,)),
        dma((4, COLS)), dma((4, COLS)),
        dma((8, 3)), dma((8,)),
        dma((2, 4)), dma((2, 4)), dma((2, 4)), dma((2, 4)),
        dma((2, COLS)), dma((2, COLS)), dma((11,)),
    ]
    mid, new = pl.pallas_call(
        kernel,
        out_shape=(jax.ShapeDtypeStruct((A, 128), BF16), jax.ShapeDtypeStruct((T, C), BF16)),
        in_specs=[pl.BlockSpec(memory_space=pl.ANY)] * len(args),
        out_specs=(pl.BlockSpec(memory_space=pl.ANY),) * 2,
        scratch_shapes=scratch,
        compiler_params=pltpu.CompilerParams(
            collective_id=0, has_side_effects=True, vmem_limit_bytes=60 * 1024 * 1024
        ),
        name="block",
    )(*args)
    hbm = pl.BlockSpec(memory_space=pl.ANY)
    return pl.pallas_call(
        to_atoms,
        out_shape=(jax.ShapeDtypeStruct((A, 128), BF16), jax.ShapeDtypeStruct((T, C), BF16)),
        in_specs=[hbm] * 4,
        out_specs=(hbm, hbm),
        scratch_shapes=[
            pltpu.VMEM((A, 128), BF16), pltpu.VMEM((T, C), BF16), pltpu.VMEM((C, 128), BF16), pltpu.VMEM((1, A), jnp.int32),
            dma((5,)), dma((3,)),
        ],
        compiler_params=pltpu.CompilerParams(vmem_limit_bytes=60 * 1024 * 1024),
        name="to_atoms",
    )(mid, new, back_weight, atok)


def solution(mesh):
    both = ("row", "col")
    in_specs = (
        P(both, None), P(both, None, None), P(both, None), P(both), P("row", None), P(None, "row", "col"), P("col"),
    ) + (P(),) * 13
    out_specs = (P(both, None), P("row", None))
    return jax.shard_map(on_device, mesh=mesh, in_specs=in_specs, out_specs=out_specs, check_vma=False)
```

```python
import functools

import jax
import jax.numpy as jnp
from jax import lax
from jax.experimental import pallas as pl
from jax.experimental.pallas import tpu as pltpu
from jax.sharding import PartitionSpec as P

F32 = jnp.float32
BF16 = jnp.bfloat16
MESH = pl.DeviceIdType.MESH
ROWS, COLS = 8, 16
EPSILON = 1e-05
MASKED = -1000000000.0
HA, DA, WQ, WK = 4, 32, 32, 128
DT = 48
REACH = 48
A = 256
T = 512
PIECES = ((0, 80), (80, 80), (160, 64), (224, 64))
K = 256
C = 768
G = 384
OWN = 32
H = 128
TOTAL_ATOMS = 32768


def dot(a, b):
    return jnp.dot(a, b, preferred_element_type=F32)


def norm(x):
    mean = jnp.mean(x, axis=-1, keepdims=True)
    d = x - mean
    var = jnp.mean(d * d, axis=-1, keepdims=True)
    return d * lax.rsqrt(var + EPSILON)


def sigmoid(x):
    return 1.0 / (1.0 + jnp.exp(-x))


def iota(shape, dim):
    return lax.broadcasted_iota(jnp.int32, shape, dim)


IN_NAMES = (
    "atoms", "abias", "kmask", "atok", "tokens", "pbias", "tmask", "aq", "akv", "ag", "ao", "pool",
    "tq", "tkv", "tg", "to", "rg", "ru", "rd",
)
EARLY = ("atoms", "akv", "aq", "ag", "kmask", "abias", "ao", "atok", "pool")
LATE = ("tokens", "tg", "tq", "tkv", "tmask", "pbias", "to", "rg", "ru", "rd")
SPANS = tuple(((DT * h) // 128, (DT * h + DT - 1) // 128 - (DT * h) // 128 + 1) for h in range(8))


def split_lse(stat):
    high = stat.astype(BF16).astype(F32)
    rest = stat - high
    middle = rest.astype(BF16).astype(F32)
    third = iota(stat.shape, 1) // 8
    return jnp.where(third == 0, high, jnp.where(third == 1, middle, rest - middle))


def join_lse():
    l_r, l_c = iota((128, 128), 0), iota((128, 128), 1)
    return jnp.where((l_r < 24) & (lax.rem(l_r, 8) == lax.rem(l_c, 8)), 1.0, 0.0).astype(BF16)


def merge(values, lse, want_lse):
    s_r, s_c = iota((128, G), 0), iota((128, G), 1)
    spread = jnp.where((s_r < 16) & (lax.rem(s_r, 8) == s_c // DT), 1.0, 0.0).astype(BF16)
    top = lse[0]
    for l in lse[1:]:
        top = jnp.maximum(top, l)
    wgt = [jnp.exp(l - top) for l in lse]
    total = wgt[0]
    for w in wgt[1:]:
        total = total + w
    inv = 1.0 / total
    first = iota(top.shape, 1) < 8
    out = None
    for w, v in zip(wgt, values):
        w = w * inv
        high = w.astype(BF16).astype(F32)
        term = dot(jnp.where(first, high, w - high).astype(BF16), spread) * v.astype(F32)
        out = term if out is None else out + term
    if want_lse:
        return jnp.concatenate([out, split_lse(top + jnp.log(total))], axis=1).astype(BF16)
    return out


def kernel(*refs):
    n_in = len(IN_NAMES)
    hbm = dict(zip(IN_NAMES, refs[:n_in]))
    mid_out, tokens_out = refs[n_in : n_in + 2]
    (
        ext, abias, kmask, tk, tokens, pbias, tmask, aq, akv, ag, ao, pool, tq, tkv, tg, to, rg, ru, rd,
        wk_t, g_mid, feats, acc, selsum, tmid, tnorm, knorm, q_s, kt_s, v_s, snd, rcv, snd2, rcv2, g_new,
        in_sem, halo_s, halo_r, mid_s, mid_r, key_s, key_r,
        one_s, one_r, two_s, two_r, new_s, new_r, own_sem,
    ) = refs[n_in + 2 :]

    r = lax.axis_index("row")
    c = lax.axis_index("col")
    y, x = c // 4, lax.rem(c, 4)
    z, core = r // 2, lax.rem(r, 2)
    lin = r * COLS + c
    nxt = lax.rem(lin + 1, ROWS * COLS)
    prv = lax.rem(lin + ROWS * COLS - 1, ROWS * COLS)
    nxt_id = (nxt // COLS, lax.rem(nxt, COLS))
    prv_id = (prv // COLS, lax.rem(prv, COLS))
    sibling = (z * 2 + 1 - core, c)

    def remote(src, dst, ss, rs, dev):
        return pltpu.make_async_remote_copy(
            src_ref=src, dst_ref=dst, send_sem=ss, recv_sem=rs, device_id=dev, device_id_type=MESH
        )

    def x_peer(i):
        return y * 4 + lax.rem(x + i, 4)

    def y_peer(i):
        return lax.rem(y + i, 4) * 4 + x

    near = (x_peer, y_peer)

    bar = pltpu.get_barrier_semaphore()
    partners = [nxt_id, prv_id, (lax.rem(z + 1, 4) * 2 + core, c), (lax.rem(z + 3, 4) * 2 + core, c)]
    partners += [(r, peer(i)) for i in (2, 1, 3) for peer in near] + [sibling]
    for dev in partners:
        pl.semaphore_signal(bar, inc=1, device_id=dev, device_id_type=MESH)

    fetch = {}
    vm = dict(
        atoms=ext.at[pl.ds(REACH, A)], abias=abias, kmask=kmask, atok=tk, tokens=tokens, pbias=pbias, tmask=tmask,
        aq=aq, akv=akv, ag=ag, ao=ao, pool=pool, tq=tq, tkv=tkv, tg=tg, to=to, rg=rg, ru=ru, rd=rd,
    )
    for i, name in enumerate(EARLY + LATE):
        fetch[name] = pltpu.make_async_copy(hbm[name], vm[name], in_sem.at[i])
    for name in EARLY:
        fetch[name].start()

    for name in ("atoms", "akv", "aq", "ag"):
        fetch[name].wait()
    own_f = ext[pl.ds(REACH, A), :].astype(F32)
    own_n = norm(own_f).astype(BF16)
    q_a = dot(own_n, aq[...]).astype(BF16)
    gate_a = sigmoid(dot(own_n, ag[...]))
    kv_own = dot(own_n, akv[...]).astype(BF16)
    fetch["kmask"].wait()
    fetch["abias"].wait()
    p_r = iota((HA * WQ, HA * WQ), 0)
    p_c = iota((HA * WQ, HA * WQ), 1)
    perm = (p_c == lax.rem(p_r, WQ) * HA + p_r // WQ).astype(F32).astype(BF16)
    bias_w = [dot(perm, abias[pl.ds(HA * WQ * w, HA * WQ), :]) for w in range(A // WQ)]
    lane = iota((1, WK), 1)
    head_f = [jnp.where((lane // DA) == h, 1.0, 0.0).astype(F32) for h in range(HA)]
    head_b = [f.astype(BF16) for f in head_f]

    def window(w, kv):
        q_w = q_a[WQ * w : WQ * (w + 1)]
        q_bd = jnp.concatenate([q_w * head_b[h] for h in range(HA)], axis=0)
        s = lax.dot_general(q_bd, kv[:, :WK], (((1,), (1,)), ((), ())), preferred_element_type=F32)
        s = s * (DA**-0.5) + bias_w[w]
        pos = lin * A + WQ * w + lane - REACH
        valid = (kmask[pl.ds(w, 1), :] == 1) & (pos >= 0) & (pos < TOTAL_ATOMS)
        s = jnp.where(valid, s, MASKED)
        e = jnp.exp(s - jnp.max(s, axis=-1, keepdims=True))
        t = jnp.sum(e, axis=-1, keepdims=True)
        o = dot(e.astype(BF16), kv[:, WK:]) / t
        return sum(o[WQ * h : WQ * (h + 1)] * head_f[h] for h in range(HA))

    def mid_of(first, attended):
        rows = slice(first, first + WQ * len(attended))
        gated = (jnp.concatenate(attended, axis=0) * gate_a[rows]).astype(BF16)
        return (own_f[rows] + dot(gated, ao[...])).astype(BF16)

    def put(piece, rows):
        g_mid[c, PIECES[piece][0] : PIECES[piece][0] + 64, :] = rows

    fetch["ao"].wait()
    inner = mid_of(64, [window(w, kv_own[WQ * w - REACH : WQ * w - REACH + WK]) for w in (2, 3, 4, 5)])
    put(0, inner[:64])
    put(1, inner[64:])
    fetch["atok"].wait()
    numbers = jnp.broadcast_to(tk[...] - r * T, (16, A))
    turned, rest = pltpu.roll(numbers[:, :H], 64, 1), numbers[:, H:]
    left = iota((16, H), 1) < 64
    line = iota((16, H), 0)
    for piece in range(2):
        number = jnp.where(left, turned, rest) if piece == 0 else jnp.where(left, rest, turned)
        number = jnp.where(line == 0, number >> 1, jnp.where(line == 1, number & 1, 0))
        g_mid[c, 64 + 80 * piece : 80 + 80 * piece, :] = number.astype(F32).astype(BF16)
    pl.semaphore_wait(bar, len(partners))

    halo = [
        remote(ext.at[pl.ds(A, REACH)], ext.at[pl.ds(0, REACH)], halo_s.at[0], halo_r.at[0], nxt_id),
        remote(ext.at[pl.ds(REACH, REACH)], ext.at[pl.ds(REACH + A, REACH)], halo_s.at[1], halo_r.at[1], prv_id),
    ]
    for cp in halo:
        cp.start()

    def mid_copy(piece, s, slot, dev):
        rows = g_mid.at[s, pl.ds(*PIECES[piece])]
        return remote(rows, rows, mid_s.at[piece, slot], mid_r.at[piece, s], (r, dev))

    def own_hops(piece, send):
        half = piece % 2
        for i in (2, 1, 3):
            send(piece, c, i - 1, near[half](i))
        for i in (2, 1, 3):
            send(piece, c, i + 2, near[1 - half](i))

    def next_hops(piece, k, wait, send):
        half = piece % 2
        s = near[half]((1, 3, 2)[k])
        if wait is not None:
            wait(piece, s, 0, c).wait_recv()
        for i in (2, 1, 3):
            send(piece, s, 3 * k + i + 5, near[1 - half](i))

    def all_hops(piece, send):
        own_hops(piece, send)
        for k in range(3):
            next_hops(piece, k, None, send)

    def mid_start(piece, s, slot, dev):
        mid_copy(piece, s, slot, dev).start()

    def onward(pieces):
        for k in range(3):
            for piece in pieces:
                next_hops(piece, k, mid_copy, mid_start)

    own_hops(0, mid_start)
    own_hops(1, mid_start)
    for name in LATE:
        fetch[name].start()
    onward((0, 1))
    edges = []
    for side in range(2):
        halo[side].wait_recv()
        edge = norm(ext[pl.ds((REACH + A) * side, REACH), :].astype(F32)).astype(BF16)
        inside = jnp.where(lin == (ROWS * COLS - 1) * side, 0.0, 1.0).astype(F32)
        edges.append((dot(edge, akv[...]) * inside).astype(BF16))
    near_by = jnp.concatenate([kv_own[6 * WQ - REACH :], edges[1]], axis=0)
    put(2, mid_of(192, [window(6, near_by[:WK]), window(7, near_by[WQ : WQ + WK])]))
    own_hops(2, mid_start)
    near_by = jnp.concatenate([edges[0], kv_own[: WK - WQ + 16]], axis=0)
    put(3, mid_of(0, [window(0, near_by[:WK]), window(1, near_by[WQ : WQ + WK])]))
    own_hops(3, mid_start)
    mid_out_copies = [
        pltpu.make_async_copy(g_mid.at[c, pl.ds(PIECES[i][0], 64)], mid_out.at[pl.ds(b, 64)], own_sem.at[i])
        for i, b in enumerate((64, 128, 192, 0))
    ]
    for cp in mid_out_copies:
        cp.start()

    fetch["tkv"].wait()
    for i in range(C // 128):
        lanes = slice(128 * i, 128 * (i + 1))
        wk_t[lanes, :] = tkv[:, lanes].astype(F32).T.astype(BF16)
    fetch["pool"].wait()

    key_off = lax.rem(c, 2) * K

    def step_blocks(step):
        o = lax.rem(step * (step + 1) // 2, 4)
        return [lax.rem(y + o, 4) * 4 + b for b in range(4)], [b * 4 + lax.rem(x + o, 4) for b in range(4)]

    def selector(late, step, off):
        at = (iota((K, H), 0) + off).astype(F32)
        left = iota((8, H), 1) < 64
        sel = []
        for half, blocks in enumerate(step_blocks(step)):
            numbers = []
            for s in blocks:
                terms = g_mid[s, 64 + 80 * half : 80 + 80 * half, :].astype(F32)
                numbers.append(jnp.broadcast_to(2.0 * terms[0:1] + terms[1:2], (8, H)))
            for n in (0, 2):
                if late:
                    pair = jnp.where(left, pltpu.roll(numbers[n], 64, 1), numbers[n + 1])
                else:
                    pair = jnp.where(left, numbers[n], pltpu.roll(numbers[n + 1], 64, 1))
                sel.append(jnp.where(at == pair[0:1], 1.0, 0.0).astype(F32))
        return sel

    def feat_rows(half, step, n):
        return pl.ds(pl.multiple_of((4 * half + step) * 512, 512), 512 * n)

    def pool_into(off, sel, f):
        rows = pl.ds(pl.multiple_of(off, K), K)
        count = sel[0]
        for m in sel[1:]:
            count = count + m
        selsum[rows, :] += count
        acc[rows, :] += dot(jnp.concatenate([m.astype(BF16) for m in sel], axis=1), f)

    def pool_step(late, wait, step, carry):
        rows = []
        for half, blocks in enumerate(step_blocks(step)):
            piece = 2 * late + half
            if wait:
                for s in blocks:
                    mid_copy(piece, s, 0, s).wait_recv()
            rows += [g_mid[s, pl.ds(PIECES[piece][0], 64), :] for s in blocks]
        f = jnp.concatenate(rows, axis=0)
        f = jnp.maximum(dot(f, pool[...]), 0.0).astype(BF16)
        feats[feat_rows(late, step, 1), :] = f
        pool_into(key_off, selector(late, step, key_off), f)
        return carry

    acc[...] = jnp.zeros(acc.shape, F32)
    selsum[...] = jnp.zeros(selsum.shape, F32)
    for late in range(2):
        pool_step(late, False, 0, 0)
        if late == 0:
            onward((2, 3))
        lax.fori_loop(1, 4, functools.partial(pool_step, late, True), 0)
    fetch["tokens"].wait()
    ones = jnp.ones((H, 128), BF16)

    def finish_chunk(first):
        rows = pl.ds(pl.multiple_of(first, 128), 128)
        inv = 1.0 / dot(selsum[rows, :].astype(BF16), ones)
        inv = jnp.concatenate([inv] * (C // 128), axis=1)
        m = (tokens[rows, :].astype(F32) + acc[rows, :] * inv).astype(BF16)
        tmid[rows, :] = m
        tnorm[rows, :] = norm(m.astype(F32)).astype(BF16)

    z0, core0 = (c // 2) // 2, lax.rem(c // 2, 2)
    away = lax.rem(z - z0 + 4, 4)
    on_core = core == core0
    is_src = on_core & (away == 0)
    is_sib = jnp.logical_not(on_core) & (away == 0)
    odd = jnp.where(on_core, 0, 1)
    swap = jnp.where(away == 3, 1, 0)
    up, down = (lax.rem(z + 1, 4) * 2 + core, c), (lax.rem(z + 3, 4) * 2 + core, c)
    onward_id = (lax.rem(z + away, 4) * 2 + core, c)

    def key_copy(q, slot, dev):
        rows = knorm.at[pl.ds(pl.multiple_of(q * OWN, OWN), OWN)]
        return remote(rows, rows, key_s.at[q, slot], key_r.at[q], dev)

    def chip_part(n):
        return 2 * lax.rem(n + 2 * swap, 4) + odd

    for pair in range(2):
        finish_chunk(key_off + 128 * pair)

        @pl.when(is_src)
        def _():
            rows = pl.ds(pl.multiple_of(key_off + 128 * pair, 128), 128)
            knorm[pl.ds(128 * pair, 128), :] = tnorm[rows, :]
            q = 4 * pair
            for p in (q + 1, q + 3):
                key_copy(p, 2, sibling).start()
            for p in (q, q + 2):
                key_copy(p, 0, up).start()
            if pair == 1:
                for p in (4, 6, 0, 2):
                    key_copy(p, 1, down).start()
            for p in (q, q + 2):
                key_copy(p, 2, sibling).start()

    @pl.when(is_sib)
    def _():
        for p in (1, 3, 5, 7):
            key_copy(p, 0, up).wait_recv()
            key_copy(p, 0, up).start()
            if p > 4:
                key_copy(p, 1, down).start()
        for p in (1, 3):
            key_copy(p, 1, down).start()

    other_off = K - key_off

    def other_step(half, step, carry):
        sel = selector(half, 2 * step, other_off) + selector(half, 2 * step + 1, other_off)
        pool_into(other_off, sel, feats[feat_rows(half, 2 * step, 2), :])
        return carry

    for half in range(2):
        lax.fori_loop(0, 2, functools.partial(other_step, half), 0)
    own_rows = pl.ds(pl.multiple_of(c * OWN, OWN), OWN)
    fetch["tq"].wait()

    def queries():
        for i in range(4):
            rows = pl.ds(128 * i, 128)
            q_s[rows, :] = dot(tnorm[rows, :], tq[...]).astype(BF16)

    between = [lambda: finish_chunk(other_off), lambda: finish_chunk(other_off + 128), queries]

    @pl.when(away == 2)
    def _():
        for work in between:
            work()

    for n in range(4):

        @pl.when(away != 0)
        def _():
            key_copy(chip_part(n), 2, sibling).wait_recv()

        if n < 2:

            @pl.when((away == 1) | (away == 3))
            def _():
                key_copy(chip_part(n), 0, onward_id).start()

        @pl.when(away != 0)
        def _():
            key_copy(chip_part(n), 2, sibling).start()

        if n < 3:
            pl.when(away != 2)(between[n])

    @pl.when(jnp.logical_not(is_src))
    def _():
        for n in range(4):
            q = 2 * n + 1 - odd
            key_copy(q, 2, sibling).wait_recv()

    kt = lax.dot_general(wk_t[...], knorm[...], (((1,), (1,)), ((), ())), preferred_element_type=F32) * (DT**-0.5)
    row_i = iota((C, 1), 0)
    v_full = dot(knorm[...], tkv[:, C:])
    lane_i = iota((1, C), 1)
    for g in range(2):
        for h in range(8):
            b0, n = SPANS[h]
            lo, hi = G * g + 128 * b0, G * g + 128 * (b0 + n)
            start = G * g + DT * h
            rm = (row_i[lo:hi] >= start) & (row_i[lo:hi] < start + DT)
            kt_s[8 * g + h, pl.ds(0, 128 * n), :] = jnp.where(rm, kt[lo:hi], 0.0).astype(BF16)
            lm = (lane_i[:, lo:hi] >= start) & (lane_i[:, lo:hi] < start + DT)
            v_s[8 * g + h, :, pl.ds(0, 128 * n)] = jnp.where(lm, v_full[:, lo:hi], 0.0).astype(BF16)
    fetch["tmask"].wait()
    fetch["pbias"].wait()

    def one_copy(g, d):
        return remote(snd.at[g, d], rcv.at[g, lax.rem(c // (1 + 3 * g), 4)], one_s.at[g, d],
                      one_r.at[g, lax.rem(c // (1 + 3 * g), 4)], (r, (y * 4 + d) * (1 - g) + (d * 4 + x) * g))

    def attend(offsets, g, carry):
        me = lax.rem(c // (1 + 3 * g), 4)
        dests = [lax.rem(me + o, 4) for o in offsets]
        size = 128 * len(dests)
        rows = [
            pl.ds(pl.multiple_of((b * (4 - 3 * g) + d * (1 + 3 * g)) * OWN, OWN), OWN) for d in dests for b in range(4)
        ]
        live = tmask[...] == 1
        lane8 = lax.rem(iota((size, 128), 1), 8)
        parts = [None] * 3
        stat = jnp.zeros((size, 128), F32)
        for h in range(8):
            b0, n = SPANS[h]
            lanes = pl.ds(pl.multiple_of(g * G + 128 * b0, 128), 128 * n)
            qw = jnp.concatenate([q_s[rw, lanes] for rw in rows], axis=0)
            s = dot(qw, kt_s[g * 8 + h, pl.ds(0, 128 * n), :])
            s = s + jnp.concatenate([pbias[g * 8 + h, rw, :] for rw in rows], axis=0).astype(F32)
            s = jnp.where(live, s, MASKED)
            top = jnp.max(s, axis=-1, keepdims=True)
            e = jnp.exp(s - top)
            total = jnp.sum(e, axis=-1, keepdims=True)
            o = dot(e.astype(BF16), v_s[g * 8 + h, :, pl.ds(0, 128 * n)]) * (1.0 / total)
            for b in range(n):
                ob = o[:, 128 * b : 128 * (b + 1)]
                parts[b0 + b] = ob if parts[b0 + b] is None else parts[b0 + b] + ob
            stat = jnp.where(lane8 == h, top + jnp.log(total), stat)
        stat = split_lse(stat)
        for n, d in enumerate(dests):
            for b in range(3):
                snd[g, d, pl.ds(128 * b, 128), :] = parts[b][128 * n : 128 * (n + 1)].astype(BF16)
            snd[g, d, pl.ds(G, 32), :] = stat[128 * n : 128 * (n + 1)].T[:32].astype(BF16)

            if offsets[n] != 0:
                one_copy(g, d).start()

        return carry

    for offsets in ((2,), (1, 3), (0,)):
        lax.fori_loop(0, 2, functools.partial(attend, offsets), 0)

    fetch["tg"].wait()
    gate_t = sigmoid(dot(tnorm[own_rows, :], tg[...]))
    mine = (x, y)
    join = join_lse()

    def two_copy(g, d):
        dev = (r, d * 4 + x) if g == 0 else (r, y * 4 + d)
        me = mine[1 - g]
        return remote(snd2.at[g, d], rcv2.at[g, me], two_s.at[g, d], two_r.at[g, me], dev)

    for g in range(2):
        blocks = [snd[g, mine[g]]]
        for i in (2, 3, 1):
            d = lax.rem(mine[g] + i, 4)
            remote(snd.at[g, d], rcv.at[g, d], one_s.at[g, d], one_r.at[g, d], (r, near[g](i))).wait_recv()
            blocks.append(rcv[g, d])
        values = [jnp.concatenate([b[128 * k : 128 * (k + 1)] for k in range(3)], axis=1) for b in blocks]
        lse = [
            lax.dot_general(b[G:], join[:32], (((0,), (0,)), ((), ())), preferred_element_type=F32) for b in blocks
        ]
        half_merged = merge(values, lse, True)
        for d in range(4):
            snd2[g, d] = half_merged[OWN * d : OWN * (d + 1)]
        for i in (2, 1, 3):
            two_copy(g, lax.rem(mine[1 - g] + i, 4)).start()
    merged = []
    for g in range(2):
        blocks = [snd2[g, mine[1 - g]]]
        for i in (1, 3, 2):
            d = lax.rem(mine[1 - g] + i, 4)
            remote(snd2.at[g, d], rcv2.at[g, d], two_s.at[g, d], two_r.at[g, d], (r, near[1 - g](i))).wait_recv()
            blocks.append(rcv2[g, d])
        merged.append(merge([b[:, :G] for b in blocks], [dot(b[:, G:], join) for b in blocks], False))
    att = jnp.concatenate(merged, axis=1)

    for name in ("to", "rg", "ru", "rd"):
        fetch[name].wait()
    gated = (att * gate_t).astype(BF16)
    t_att = (tmid[own_rows, :].astype(F32) + dot(gated, to[...])).astype(BF16)
    n_att = norm(t_att.astype(F32)).astype(BF16)
    up = dot(n_att, rg[...])
    hid = (up * sigmoid(up) * dot(n_att, ru[...])).astype(BF16)
    t_new = (t_att.astype(F32) + dot(hid, rd[...])).astype(BF16)
    g_new[own_rows, :] = t_new

    def rows_of(half, s):
        return pl.ds(pl.multiple_of(s * OWN + 16 * half, 16), 16)

    def new_copy(half, s, slot, dev):
        dst = g_new if slot < 3 else tokens_out
        return remote(
            g_new.at[rows_of(half, s)], dst.at[rows_of(half, s)], new_s.at[half, slot], new_r.at[half, s], (r, dev)
        )

    out_copies = [pltpu.make_async_copy(g_new.at[own_rows], tokens_out.at[own_rows], own_sem.at[4])]
    def new_start(half, s, slot, dev):
        new_copy(half, s, slot, dev).start()

    for half in range(2):
        own_hops(half, new_start)
    out_copies[0].start()
    for half in range(2):
        for k, i in enumerate((1, 3, 2)):
            rows = rows_of(half, near[half](i))
            out_copies.append(pltpu.make_async_copy(g_new.at[rows], tokens_out.at[rows], own_sem.at[5 + 3 * half + k]))

    for k in range(3):
        for half in range(2):
            next_hops(half, k, new_copy, new_start)
    for cp in out_copies[1:]:
        cp.start()

    for cp in halo:
        cp.wait_send()

    for piece in range(4):
        all_hops(piece, lambda *a: mid_copy(*a).wait_send())
    for g in range(2):
        for i in (1, 3, 2):
            one_copy(g, lax.rem(mine[g] + i, 4)).wait_send()
            two_copy(g, lax.rem(mine[1 - g] + i, 4)).wait_send()

    @pl.when(is_src)
    def _():
        for q in range(8):
            key_copy(q, 2, sibling).wait_send()
            if q % 2 == 0:
                key_copy(q, 0, up).wait_send()
                key_copy(q, 1, down).wait_send()

    @pl.when(is_sib)
    def _():
        for q in (1, 3, 5, 7):
            key_copy(q, 0, up).wait_send()
            key_copy(q, 1, down).wait_send()

    @pl.when(away != 0)
    def _():
        for n in range(4):
            key_copy(chip_part(n), 2, sibling).wait_send()

    @pl.when((away == 1) | (away == 3))
    def _():
        for n in (0, 1):
            key_copy(chip_part(n), 0, onward_id).wait_send()

    for half in range(2):
        for i in (1, 3, 2):
            for j in range(4):
                s = y_peer(i) // 4 * 4 + j if half == 0 else j * 4 + lax.rem(x + i, 4)
                new_copy(half, s, 3, s).wait_recv()
    for cp in mid_out_copies + out_copies:
        cp.wait()
    for half in range(2):
        all_hops(half, lambda *a: new_copy(*a).wait_send())


def to_atoms(mid, new, back, atok, atoms_out, tokens_out, mid_v, new_v, back_v, atok_v, in_sem, out_sem):
    n = 2
    rows = [pl.ds(i * (T // n), T // n) for i in range(n)]
    ins = [pltpu.make_async_copy(new.at[w], new_v.at[w], in_sem.at[i]) for i, w in enumerate(rows)]
    small = [
        pltpu.make_async_copy(a, b, in_sem.at[n + i])
        for i, (a, b) in enumerate(((atok, atok_v), (back, back_v), (mid, mid_v)))
    ]
    outs = [pltpu.make_async_copy(new_v.at[w], tokens_out.at[w], out_sem.at[i]) for i, w in enumerate(rows)]
    for cp in ins[:1] + small + ins[1:]:
        cp.start()
    first = lax.axis_index("row") * T
    lane = iota((A, 128), 1).astype(F32)
    ins[0].wait()
    outs[0].start()
    for cp in small:
        cp.wait()
    tok_t = jnp.broadcast_to((atok_v[...] - first).astype(F32), (128, A)).T
    update = None
    for i, w in enumerate(rows):
        if i > 0:
            ins[i].wait()
            outs[i].start()
        for at in range(T // n * i, T // n * (i + 1), 128):
            pick = jnp.where(tok_t == lane + float(at), 1.0, 0.0).astype(BF16)
            term = dot(pick, dot(new_v[pl.ds(at, 128), :], back_v[...]).astype(BF16))
            update = term if update is None else update + term
    mid_v[...] = (mid_v[...].astype(F32) + update).astype(BF16)
    last = pltpu.make_async_copy(mid_v, atoms_out, out_sem.at[n])
    last.start()
    for cp in outs + [last]:
        cp.wait()


def on_device(
    atoms, atom_bias, key_mask, atom_token, tokens, pair_bias, token_mask,
    atom_query, atom_keyval, atom_gate, atom_out, pool_weight,
    token_query, token_keyval, token_gate, token_out, trans_gate, trans_up, trans_down, back_weight,
):
    atok = atom_token.reshape(1, A)
    args = (
        atoms, atom_bias.reshape(A * HA, WK), key_mask, atok, tokens, pair_bias,
        token_mask.reshape(1, K), atom_query, atom_keyval, atom_gate, atom_out, pool_weight,
        token_query, token_keyval, token_gate, token_out, trans_gate, trans_up, trans_down,
    )
    vmem = [pltpu.VMEM(a.shape, a.dtype) for a in args]
    vmem[0] = pltpu.VMEM((A + 2 * REACH, 128), BF16)
    dma = pltpu.SemaphoreType.DMA
    scratch = vmem + [
        pltpu.VMEM((C, C), BF16),
        pltpu.VMEM((COLS, A + 32, 128), BF16),
        pltpu.VMEM((COLS * A, C), BF16),
        pltpu.VMEM((T, C), F32),
        pltpu.VMEM((T, H), F32),
        pltpu.VMEM((T, C), BF16),
        pltpu.VMEM((T, C), BF16),
        pltpu.VMEM((K, C), BF16),
        pltpu.VMEM((T, C), BF16),
        pltpu.VMEM((16, 256, K), BF16),
        pltpu.VMEM((16, K, 256), BF16),
        pltpu.VMEM((2, 4, G + 32, 128), BF16),
        pltpu.VMEM((2, 4, G + 32, 128), BF16),
        pltpu.VMEM((2, 4, OWN, G + 128), BF16),
        pltpu.VMEM((2, 4, OWN, G + 128), BF16),
        pltpu.VMEM((T, C), BF16),
        dma((len(args),)), dma((2,)), dma((2,)),
        dma((4, COLS)), dma((4, COLS)),
        dma((8, 3)), dma((8,)),
        dma((2, 4)), dma((2, 4)), dma((2, 4)), dma((2, 4)),
        dma((2, COLS)), dma((2, COLS)), dma((11,)),
    ]
    mid, new = pl.pallas_call(
        kernel,
        out_shape=(jax.ShapeDtypeStruct((A, 128), BF16), jax.ShapeDtypeStruct((T, C), BF16)),
        in_specs=[pl.BlockSpec(memory_space=pl.ANY)] * len(args),
        out_specs=(pl.BlockSpec(memory_space=pl.ANY),) * 2,
        scratch_shapes=scratch,
        compiler_params=pltpu.CompilerParams(
            collective_id=0, has_side_effects=True, vmem_limit_bytes=60 * 1024 * 1024
        ),
        name="block",
    )(*args)
    hbm = pl.BlockSpec(memory_space=pl.ANY)
    return pl.pallas_call(
        to_atoms,
        out_shape=(jax.ShapeDtypeStruct((A, 128), BF16), jax.ShapeDtypeStruct((T, C), BF16)),
        in_specs=[hbm] * 4,
        out_specs=(hbm, hbm),
        scratch_shapes=[
            pltpu.VMEM((A, 128), BF16), pltpu.VMEM((T, C), BF16), pltpu.VMEM((C, 128), BF16), pltpu.VMEM((1, A), jnp.int32),
            dma((5,)), dma((3,)),
        ],
        compiler_params=pltpu.CompilerParams(vmem_limit_bytes=60 * 1024 * 1024),
        name="to_atoms",
    )(mid, new, back_weight, atok)


def solution(mesh):
    both = ("row", "col")
    in_specs = (
        P(both, None), P(both, None, None), P(both, None), P(both), P("row", None), P(None, "row", "col"), P("col"),
    ) + (P(),) * 13
    out_specs = (P(both, None), P("row", None))
    return jax.shard_map(on_device, mesh=mesh, in_specs=in_specs, out_specs=out_specs, check_vma=False)
```
